128 devices in a mesh: grp: 2 (over x_hi), sp: 64 (over y, z, x_lo, core).
Axes of the slice: x: 4 (x_hi: 2, x_lo: 2; x = x_hi * 2 + x_lo), y: 4, z: 4, core: 2. Of those that a mesh axis runs over, the one named last changes fastest.
Arguments:
- positions: float32 [3, 262144], P(None, ('grp', 'sp')), may hold values from 0 to 2
- dipoles: float32 [3, 262144], P(None, ('grp', 'sp')), may hold values from -6 to 6
- spline_values: float32 [3, 4, 262144], P(None, None, ('grp', 'sp')), may hold values from 0 to 1
- spline_slopes: float32 [3, 4, 262144], P(None, None, ('grp', 'sp')), may hold values from -5 to 5
- plane_base: int32 [262144], P(('grp', 'sp')), may hold values from 0 to 383, as said below
- row_base: int32 [262144], P(('grp', 'sp')), may hold values from 0 to 255
- column_base: int32 [262144], P(('grp', 'sp')), may hold values from 0 to 255
- pair_home: int32 [4096], P(('grp', 'sp')), may hold values from 0 to 15
- pair_other: int32 [4096], P(('grp', 'sp')), may hold values from 0 to 47, as said below
- pair_count: int32 [128], P(('grp', 'sp')), may hold values from 6 to 32, as said below
- influence: float32 [384, 256, 256], P(None, ('grp', 'sp')), may hold values from 0.05 to 1
Outputs:
- field: float32 [3, 262144], P(None, ('grp', 'sp'))
The draws below stay inside these ranges and needn't reach their ends.
Inputs may be any that keep to these rules, and one draw needn't show every extreme that they name: The atoms of cell d have plane_base from d * 3 to (d + 1) * 3 - 1. `pair_other`: slot t of a cell takes its source cluster from the lower neighbour cell, the own cell or the upper neighbour cell as t mod 3 is 0, 1 or 2. Slots d * 32 to d * 32 + pair_count[d] - 1 of cell d are live, the rest are ignored; some cell has all 32 slots live.
All inputs are finite; a program needn't handle non-finite values.
Results may differ from the reference program's by a relative error of at most 0.0003.
Values sent between devices are 32-bit elements; how exact they have to be, the bound alone decides.
A program may use at most 64 MiB of HBM per device.

```python
import math
import jax
import jax.numpy as jnp
from jax import lax

CL = 128
CLU_DEV = 16
PAIR_DEV = 32
GX = 384
GY = 256
GZ = 256
PLANES = 3
ATOM_DEV = 2048
ATOMS = 262144
PAIRS = 4096
N_GRP = 2
N_SP = 64


def draw_plane_base(key, part):
    key = jax.random.fold_in(key, 11)
    owner = jnp.arange(ATOMS, dtype=jnp.int32) // ATOM_DEV
    return owner * PLANES + jax.random.randint(key, (ATOMS,), 0, PLANES, dtype=jnp.int32)


def draw_pair_other(key, part):
    key = jax.random.fold_in(key, 37)
    slot = jnp.arange(PAIRS, dtype=jnp.int32) % PAIR_DEV
    return (slot % 3 * CLU_DEV + jax.random.randint(key, (PAIRS,), 0, CLU_DEV, dtype=jnp.int32)).astype(jnp.int32)


def draw_pair_count(key, part):
    key = jax.random.fold_in(key, 23)
    first_key, second_key = jax.random.split(key)
    devices = N_GRP * N_SP
    divisor = 1 + jax.random.randint(first_key, (devices,), 0, 5, dtype=jnp.int32)
    counts = PAIR_DEV // divisor
    fullest = jax.random.randint(second_key, (), 0, devices, dtype=jnp.int32)
    return jnp.where(jnp.arange(devices, dtype=jnp.int32) == fullest, PAIR_DEV, counts).astype(jnp.int32)


def set_ends(array, rng, least, top_value):
    longest = array.shape.index(max(array.shape))
    spots = []
    for shift in (0, 1):
        where = [jax.random.randint(jax.random.fold_in(rng, axis), (), 0, length) for axis, length in enumerate(array.shape)]
        where[longest] = (where[longest] + shift) % array.shape[longest]
        spots.append(tuple(where))
    return array.at[spots[0]].set(least).at[spots[1]].set(top_value)


def block_scale(stream_key, extent, shards, smallest, high):
    loudness, own = 1.0, jax.random.fold_in(stream_key, 6)
    for position, shards_of in shards:
        heights = jnp.exp(jax.random.uniform(jax.random.fold_in(own, position), (shards_of,), jnp.float32, smallest / len(shards), high / len(shards)))
        loudness = loudness * jnp.repeat(heights, extent[position] // shards_of).reshape([-1 if axis == position else 1 for axis in range(len(extent))])
    return loudness


def normal_values(key, dims, scale, bound, shards=(), kind=jnp.bfloat16):
    array = scale * jax.random.normal(key, dims, jnp.float32)
    if shards:
        array = array * block_scale(key, dims, shards, -0.22, 0.18)
    return jnp.clip(array, -bound, bound).astype(kind)


def setup_inputs(seed: int = 0) -> dict:
    splits = jax.random.split(jax.random.key(seed), 12)
    positions = jnp.clip(2.0 * jax.random.uniform(splits[0], (3, ATOMS), jnp.float32) ** block_scale(splits[0], (3, ATOMS), ((1, 128),), -0.2, 0.2), 0.0, 2.0)
    dipoles = normal_values(splits[1], (3, ATOMS), 1.0, 6.0, ((1, 128),), jnp.float32)
    spline_values = jnp.clip(1.0 * jax.random.uniform(splits[2], (3, 4, ATOMS), jnp.float32) ** block_scale(splits[2], (3, 4, ATOMS), ((2, 128),), -0.2, 0.2), 0.0, 1.0)
    spline_slopes = normal_values(splits[3], (3, 4, ATOMS), 1.0, 5.0, ((2, 128),), jnp.float32)
    plane_base = draw_plane_base(jax.random.fold_in(splits[11], 71), 0)
    row_base = set_ends(jax.random.randint(splits[5], (ATOMS,), 0, GY), jax.random.fold_in(splits[5], 1), 0, GY - 1).astype(jnp.int32)
    column_base = set_ends(jax.random.randint(splits[6], (ATOMS,), 0, GZ), jax.random.fold_in(splits[6], 1), 0, GZ - 1).astype(jnp.int32)
    pair_home = set_ends(jax.random.randint(splits[7], (PAIRS,), 0, CLU_DEV), jax.random.fold_in(splits[7], 1), 0, CLU_DEV - 1).astype(jnp.int32)
    pair_other = draw_pair_other(jax.random.fold_in(splits[11], 71), 0)
    pair_count = draw_pair_count(jax.random.fold_in(splits[11], 71), 0)
    influence = jnp.clip(jnp.exp(math.log(1.0) - 2.9957323 * jax.random.uniform(splits[10], (GX, GY, GZ), jnp.float32) ** block_scale(splits[10], (GX, GY, GZ), ((1, 128),), -0.2, 0.2)), 0.05, 1.0)
    return dict(positions=positions, dipoles=dipoles, spline_values=spline_values, spline_slopes=spline_slopes, plane_base=plane_base, row_base=row_base, column_base=column_base, pair_home=pair_home, pair_other=pair_other, pair_count=pair_count, influence=influence)


soften = 0.25
cell_width = 2.0
direct_scale = 0.125
slot_batch = 16

def block_field(home_rows, other_rows, self_mask):
    delta = [home_rows[..., axis_index, :, None] - other_rows[..., axis_index, None, :] for axis_index in range(3)]
    distance = delta[0] * delta[0] + delta[1] * delta[1] + delta[2] * delta[2]
    screen = jnp.exp(-0.5 * distance)
    inverse = lax.rsqrt(distance + soften)
    first = screen * inverse * inverse * inverse
    second = 3.0 * first * inverse * inverse
    width = home_rows.shape[-1]
    keeping = 1.0 - self_mask[..., None, None] * jnp.eye(width, dtype=jnp.float32)
    moment = [other_rows[..., 3 + axis_index, None, :] for axis_index in range(3)]
    along = delta[0] * moment[0] + delta[1] * moment[1] + delta[2] * moment[2]
    fields = [lax.optimization_barrier(jnp.sum(keeping * (second * along * delta[axis_index] - first * moment[axis_index]), axis=-1)) for axis_index in range(3)]
    return jnp.stack(fields, axis=-2)

def stencil_weights(values, slopes, offset):
    weight_x = slopes[0, offset][None, None, :] * values[1][:, None, :] * values[2][None, :, :]
    weight_y = values[0, offset][None, None, :] * slopes[1][:, None, :] * values[2][None, :, :]
    weight_z = values[0, offset][None, None, :] * values[1][:, None, :] * slopes[2][None, :, :]
    return (weight_x, weight_y, weight_z)

def stencil_cells(plane, row_base, column_base):
    steps_four = jnp.arange(4, dtype=jnp.int32)[:, None]
    rows_all = (row_base[None, :] + steps_four) % GY
    columns_all = (column_base[None, :] + steps_four) % GZ
    return (plane[None, None, :] * GY + rows_all[:, None, :]) * GZ + columns_all[None, :, :]

def reference(positions, dipoles, spline_values, spline_slopes, plane_base, row_base, column_base, pair_home, pair_other, pair_count, influence):
    devices = N_GRP * N_SP
    stacked = jnp.concatenate([positions, dipoles], axis=0)

    def device_direct(device):
        pieces = []
        for neighbour, offset in ((-1, -cell_width), (0, 0.0), (1, cell_width)):
            source = ((device + neighbour) % devices).astype(jnp.int32)
            piece = lax.dynamic_slice_in_dim(stacked, source * ATOM_DEV, ATOM_DEV, 1)
            pieces.append(piece.at[0].add(offset))
        extended = jnp.concatenate(pieces, axis=1)
        cluster_rows = extended.reshape(6, 3 * CLU_DEV, CL).transpose(1, 0, 2)
        homes = lax.dynamic_slice_in_dim(pair_home, device * PAIR_DEV, PAIR_DEV).reshape(-1, slot_batch)
        others = lax.dynamic_slice_in_dim(pair_other, device * PAIR_DEV, PAIR_DEV).reshape(-1, slot_batch)
        slot_total = pair_count[device]
        starts = jnp.arange(homes.shape[0], dtype=jnp.int32) * slot_batch

        def one_batch(operands):
            home_ids, other_ids, start = operands
            live_mask = (start + jnp.arange(slot_batch, dtype=jnp.int32) < slot_total).astype(jnp.float32)
            self_mask = (other_ids == home_ids + CLU_DEV).astype(jnp.float32)
            blocks = block_field(cluster_rows[home_ids + CLU_DEV], cluster_rows[other_ids], self_mask)
            return blocks * live_mask[:, None, None]
        blocks = lax.map(one_batch, (homes, others, starts))
        totals = jnp.zeros((CLU_DEV, 3, CL), jnp.float32).at[homes.reshape(-1)].add(blocks.reshape(-1, 3, CL))
        return totals.transpose(1, 0, 2).reshape(3, ATOM_DEV)
    direct = lax.map(device_direct, jnp.arange(devices, dtype=jnp.int32))
    direct = direct.transpose(1, 0, 2).reshape(3, ATOMS)
    grid = jnp.zeros((GX * GY * GZ,), jnp.float32)
    for offset in range(4):
        weight_x, weight_y, weight_z = stencil_weights(spline_values, spline_slopes, offset)
        cells = stencil_cells((plane_base + offset) % GX, row_base, column_base)
        grid = grid.at[cells].add(dipoles[0] * weight_x + dipoles[1] * weight_y + dipoles[2] * weight_z)
    spectrum = jnp.fft.fftn(grid.reshape(GX, GY, GZ))
    potential = jnp.real(jnp.fft.ifftn(spectrum * influence)).reshape(-1)
    recip = [jnp.zeros((ATOMS,), jnp.float32) for component in range(3)]
    for offset in range(4):
        weights = stencil_weights(spline_values, spline_slopes, offset)
        cells = stencil_cells((plane_base + offset) % GX, row_base, column_base)
        sampled = potential[cells]
        for component in range(3):
            recip[component] = recip[component] - lax.optimization_barrier(jnp.sum(weights[component] * sampled, axis=(0, 1)))
    return direct_scale * direct + jnp.stack(recip)
```

```python
import functools

import jax
import jax.numpy as jnp
import numpy as np
from jax import lax
from jax.experimental import pallas as pl
from jax.experimental.pallas import tpu as pltpu
from jax.sharding import PartitionSpec as P

CL = 128
CLU_DEV = 16
GX = 384
GY = 256
GZ = 256
DEV = 128
ATOM_DEV = 2048
SLOTS = 32
CHUNK = 512
AXES = ("grp", "sp")

f32, bf16 = jnp.float32, jnp.bfloat16
VM = pl.BlockSpec(memory_space=pltpu.VMEM)
SM = pl.BlockSpec(memory_space=pltpu.SMEM)


def halves(table):
    high = table.astype(bf16)
    low = (table - high.astype(np.float64)).astype(bf16)
    return high, low


@functools.cache
def tables():
    d = np.arange(128)[:, None]
    y = np.arange(GY)[None, :]
    angle = 2 * np.pi * ((d * y) % GY) / GY
    real, imag = np.cos(angle), -np.sin(angle)
    imag[0] = 1 - 2 * (np.arange(GY) % 2)
    forward_y = np.concatenate([real, imag], 0)
    scale = np.full((1, 256), 2.0)
    scale[0, 0] = scale[0, 128] = 1.0
    backward_y = forward_y.T * scale / (GX * GY * GZ)
    z = np.arange(GZ)
    angle = 2 * np.pi * ((z[:, None] * z[None, :]) % GZ) / GZ
    cos, sin = np.cos(angle), np.sin(angle)
    forward_z = np.block([[cos, -sin], [sin, cos]])
    backward_z = np.block([[cos, sin], [-sin, cos]])
    k = np.arange(GX)
    forward_x = []
    for p in range(3):
        angle = 2 * np.pi * ((k[:, None] * (3 * np.arange(128)[None, :] + p)) % GX) / GX
        forward_x += [np.cos(angle), np.sin(angle)]
    backward_x = np.concatenate(
        [np.concatenate([forward_x[2 * p].T, forward_x[2 * p + 1].T], 1) for p in range(3)], 0
    )
    forward_x = np.concatenate(forward_x, 1)
    out = []
    for table in (forward_y, forward_x, forward_z, backward_z, backward_x, backward_y):
        out += list(halves(table))
    return out


def split(x):
    high = x.astype(bf16)
    return high, (x - high.astype(f32)).astype(bf16)


def nn(a, b):
    return lax.dot_general(a, b, (((1,), (0,)), ((), ())), preferred_element_type=f32)


def nt(a, b):
    return lax.dot_general(a, b, (((1,), (1,)), ((), ())), preferred_element_type=f32)


def left(table_high, table_low, x):
    high, low = split(x)
    return nn(
        jnp.concatenate([table_high, table_high, table_low], 1),
        jnp.concatenate([high, low, high], 0),
    )


def right(x, table_high, table_low):
    high, low = split(x)
    return nn(
        jnp.concatenate([high, low, high], 1),
        jnp.concatenate([table_high, table_high, table_low], 0),
    )


def dense(base, weights):
    n = base.shape[1]
    step = (lax.broadcasted_iota(jnp.int32, (256, n), 0) - base) & 255
    at = [step == k for k in range(4)]
    out = []
    for w in weights:
        r = jnp.where(at[3], w[3], 0.0)
        for k in (2, 1, 0):
            r = jnp.where(at[k], w[k], r)
        out.append(r)
    return out


def atoms(ref, start, n):
    cols = pl.ds(pl.multiple_of(start, n), n)
    g = lambda r: ref[r : r + 1, cols]
    code, column = g(30).astype(jnp.int32), g(31).astype(jnp.int32)
    moment = [g(3 + i) for i in range(3)]
    v = [[g(6 + 4 * i + k) for k in range(4)] for i in range(3)]
    s = [[g(18 + 4 * i + k) for k in range(4)] for i in range(3)]
    return code & 255, column, code >> 8, moment, v, s


def plane_weights(local, w, shift):
    out = []
    for p in range(3):
        step = p + shift - local
        r = jnp.zeros_like(w[0])
        for k in range(4):
            r = jnp.where(step == k, w[k], r)
        out.append(r)
    return out


def spread_chunk(ref, start, shift, grid):
    row, column, local, m, v, s = atoms(ref, start, CHUNK)
    v2, s2 = dense(column, [v[2], s[2]])
    v1, s1 = dense(row, [v[1], s[1]])
    x0 = plane_weights(local, v[0], shift)
    xs = plane_weights(local, s[0], shift)
    a = jnp.concatenate([v1 * (m[0] * xs[p]) + s1 * (m[1] * x0[p]) for p in range(3)], 0)
    b = jnp.concatenate([v1 * (m[2] * x0[p]) for p in range(3)], 0)
    ah, al = split(a)
    bh, bl = split(b)
    vh, vl = split(v2)
    sh, sl = split(s2)
    grid[...] += nt(
        jnp.concatenate([ah, bh, ah, al, bh, bl], 1), jnp.concatenate([vh, sh, vl, vh, sl, sh], 1)
    )


def spread_kernel(own, before, grid):
    grid[...] = jnp.zeros_like(grid)

    def body(i, c):
        spread_chunk(own, i * CHUNK, 0, grid)
        spread_chunk(before, i * CHUNK, 3, grid)
        return c

    lax.fori_loop(0, ATOM_DEV // CHUNK, body, 0)


def sample_chunk(ref, start, shift, stacked, out):
    row, column, local, m, v, s = atoms(ref, start, CHUNK)
    v2, s2 = dense(column, [v[2], s[2]])
    v1, s1 = dense(row, [v[1], s[1]])
    x0 = plane_weights(local, v[0], shift)
    xs = plane_weights(local, s[0], shift)
    vh, vl = split(v2)
    sh, sl = split(s2)
    pot = stacked[...]
    tv = nn(pot, jnp.concatenate([vh, vl, vh], 0))
    ts = nn(pot, jnp.concatenate([sh, sl, sh], 0))
    tv = [tv[p * 256 : p * 256 + 256] for p in range(3)]
    ts = [ts[p * 256 : p * 256 + 256] for p in range(3)]
    ax = tv[0] * xs[0] + tv[1] * xs[1] + tv[2] * xs[2]
    ay = tv[0] * x0[0] + tv[1] * x0[1] + tv[2] * x0[2]
    az = ts[0] * x0[0] + ts[1] * x0[1] + ts[2] * x0[2]
    r = [jnp.sum(w * t, 0, keepdims=True) for w, t in ((v1, ax), (s1, ay), (v1, az))]
    out[:, pl.ds(pl.multiple_of(start, CHUNK), CHUNK)] = -jnp.concatenate(r, 0)


def sample_kernel(own, before, pot, out_own, out_before, stacked):
    high, low = split(pot[...])
    stacked[:, 0:256] = high
    stacked[:, 256:512] = high
    stacked[:, 512:768] = low

    def body(i, c):
        sample_chunk(before, i * CHUNK, 3, stacked, out_before)
        sample_chunk(own, i * CHUNK, 0, stacked, out_own)
        return c

    lax.fori_loop(0, ATOM_DEV // CHUNK, body, 0)


def direct_kernel(home, other, count, own, before, after, out, ext, acc):
    for part, ref in enumerate((before, own, after)):
        shift = 2.0 * (part - 1)
        for c in range(CLU_DEV):
            x = ref[0:8, c * CL : (c + 1) * CL]
            if part != 1:
                x = x + jnp.where(lax.broadcasted_iota(jnp.int32, (8, CL), 0) == 0, shift, 0.0)
            ext[part * CLU_DEV + c] = x
    acc[...] = jnp.zeros_like(acc)
    eye = (
        lax.broadcasted_iota(jnp.int32, (CL, CL), 0) == lax.broadcasted_iota(jnp.int32, (CL, CL), 1)
    ).astype(f32)
    which = lax.broadcasted_iota(jnp.int32, (CLU_DEV, 8, CL), 0)

    def slot(t, carry):
        h, o = home[t], other[t]
        hx = ext[h + CLU_DEV]
        ox = ext[o].T
        delta = [hx[a : a + 1, :] - ox[:, a : a + 1] for a in range(3)]
        m = [ox[:, 3 + a : 4 + a] for a in range(3)]
        q = delta[0] * delta[0] + delta[1] * delta[1] + delta[2] * delta[2]
        inverse = lax.rsqrt(q + 0.25)
        square = inverse * inverse
        self_slot = jnp.where(o == h + CLU_DEV, 1.0, 0.0)
        first = jnp.exp(-0.5 * q) * (inverse * square) * (1.0 - self_slot * eye)
        second = 3.0 * first * square
        along = second * (delta[0] * m[0] + delta[1] * m[1] + delta[2] * m[2])
        e = [jnp.sum(along * delta[a] - first * m[a], 0, keepdims=True) for a in range(3)]
        live = jnp.where(t < count[0], 0.125, 0.0)
        e = jnp.concatenate(e + [jnp.zeros((5, CL), f32)], 0) * live
        acc[...] += jnp.where(which == h, e[None], 0.0)
        return carry

    lax.fori_loop(0, SLOTS, slot, 0)
    for c in range(CLU_DEV):
        out[:, c * CL : (c + 1) * CL] = acc[c][0:3]


def device_id(t):
    return (t // 64, lax.rem(t, 64))


def exchange_start(me, p, src, dst, send_sem, recv_sem):
    def send(i, c):
        t = lax.rem(me + i, DEV)
        pltpu.make_async_remote_copy(
            src_ref=src.at[p, t],
            dst_ref=dst.at[p, me],
            send_sem=send_sem.at[p],
            recv_sem=recv_sem.at[p],
            device_id=device_id(t),
            device_id_type=pl.DeviceIdType.MESH,
        ).start()
        return c

    lax.fori_loop(1, DEV, send, 0)
    dst[p, pl.ds(me, 1)] = src[p, pl.ds(me, 1)]


def exchange_wait(p, src, sem):
    part = src.at[p, pl.ds(0, DEV - 1)]
    pltpu.make_async_copy(part, part, sem.at[p]).wait()


def to_rows(ref, p, value):
    view = ref.at[p].reshape(512, 128)
    for c in range(2):
        for h in range(2):
            view[pl.ds(2 * c + h, 128, stride=4), :] = value[
                c * 128 : c * 128 + 128, h * 128 : h * 128 + 128
            ]


def from_rows(ref, p):
    view = ref.at[p].reshape(512, 128)
    part = [view[pl.ds(k, 128, stride=4), :] for k in range(4)]
    return jnp.concatenate(part[0:2], 1), jnp.concatenate(part[2:4], 1)


def mesh_kernel(
    grid, keep, turn, fyh, fyl, fxh, fxl, fzh, fzl, bzh, bzl, bxh, bxl, byh, byl, pot,
    send1, recv1, send2, recv2, spec, ss1, rs1, ss2, rs2,
):
    me = lax.axis_index("grp") * 64 + lax.axis_index("sp")
    barrier = pltpu.get_barrier_semaphore()

    def greet(i, c):
        pl.semaphore_signal(
            barrier, inc=1, device_id=device_id(lax.rem(me + i, DEV)), device_id_type=pl.DeviceIdType.MESH
        )
        return c

    lax.fori_loop(1, DEV, greet, 0)
    pl.semaphore_wait(barrier, DEV - 1)
    for p in range(3):
        to_rows(send1, p, left(fyh[...], fyl[...], grid[p * 256 : p * 256 + 256, :]))
        exchange_start(me, p, send1, recv1, ss1, rs1)

    def forward(sign):
        total = jnp.zeros((GX, 512), f32)
        for p in range(3):
            real, imag = from_rows(recv1, p)
            imag = imag * sign
            x = jnp.concatenate(
                [jnp.concatenate([real, imag], 1), jnp.concatenate([imag, -real], 1)], 0
            )
            cols = slice(p * 256, p * 256 + 256)
            total = total + left(fxh[:, cols], fxl[:, cols], x)
        return right(total, fzh[...], fzl[...])

    for p in range(3):
        exchange_wait(p, recv1, rs1)
    spec[...] = forward(1.0) * jnp.concatenate([keep[...], keep[...]], 1)

    @pl.when(me == 0)
    def _():
        spec[...] += forward(-1.0) * jnp.concatenate([turn[...], turn[...]], 1)

    back = right(spec[...], bzh[...], bzl[...])
    real, imag = back[:, 0:256], back[:, 256:512]
    x = jnp.concatenate([jnp.concatenate([real, imag], 1), jnp.concatenate([-imag, real], 1)], 0)
    high, low = split(x)
    x = jnp.concatenate([high, low, high], 0)
    for p in range(3):
        rows = slice(p * 128, p * 128 + 128)
        y = nn(jnp.concatenate([bxh[rows, :], bxh[rows, :], bxl[rows, :]], 1), x)
        to_rows(send2, p, jnp.concatenate([y[:, 0:256], y[:, 256:512]], 0))
        exchange_start(me, p, send2, recv2, ss2, rs2)
    for p in range(3):
        exchange_wait(p, recv2, rs2)
        real, imag = from_rows(recv2, p)
        pot[p * 256 : p * 256 + 256, :] = left(byh[...], byl[...], jnp.concatenate([real, imag], 0))
    for p in range(3):
        exchange_wait(p, send1, ss1)
        exchange_wait(p, send2, ss2)


def negated(x):
    return jnp.roll(x[::-1, ::-1], (1, 1), (0, 1))


def on_device(
    positions,
    dipoles,
    spline_values,
    spline_slopes,
    plane_base,
    row_base,
    column_base,
    pair_home,
    pair_other,
    pair_count,
    influence,
):
    up = [(i, (i + 1) % DEV) for i in range(DEV)]
    down = [(j, i) for i, j in up]
    me = lax.axis_index("grp") * 64 + lax.axis_index("sp")
    near = jnp.concatenate([positions, dipoles], axis=0)
    local = plane_base % 3
    own = jnp.concatenate(
        [
            near,
            spline_values.reshape(12, ATOM_DEV),
            spline_slopes.reshape(12, ATOM_DEV),
            (row_base + 256 * local).astype(f32)[None],
            column_base.astype(f32)[None],
        ],
        axis=0,
    )
    before = lax.ppermute(own, AXES, up)
    after = lax.ppermute(near, AXES, down)
    row0, row1 = influence[:, 0, :], influence[:, 1, :]
    lower = me < 64
    sent1 = lax.ppermute(
        jnp.where(lower, row0, row1), AXES, [(e, 2 * e if e < 64 else 255 - 2 * e) for e in range(DEV)]
    )
    sent2 = lax.ppermute(
        jnp.where(lower, row1, row0),
        AXES,
        [(e, 2 * e + 1 if e < 64 else (256 - 2 * e) % DEV) for e in range(DEV)],
    )
    even = me % 2 == 0
    u, v = jnp.where(even, sent1, sent2), jnp.where(even, sent2, sent1)
    nu, nv = negated(u), negated(v)
    first = me == 0
    keep = jnp.where(first, 0.25 * ((u + nu) + (v + nv)), 0.5 * (u + nv))
    turn = jnp.where(first, 0.25 * ((u + nu) - (v + nv)), 0.0)
    limit = pltpu.CompilerParams(vmem_limit_bytes=50 << 20)
    grid = pl.pallas_call(
        spread_kernel,
        out_shape=jax.ShapeDtypeStruct((768, 256), f32),
        in_specs=[VM] * 2,
        out_specs=VM,
        compiler_params=limit,
        name="spread",
    )(own, before)
    pot = pl.pallas_call(
        mesh_kernel,
        out_shape=jax.ShapeDtypeStruct((768, 256), f32),
        in_specs=[VM] * 15,
        out_specs=VM,
        scratch_shapes=[pltpu.VMEM((3, DEV, 4, 128), f32)] * 4
        + [pltpu.VMEM((GX, 512), f32)]
        + [pltpu.SemaphoreType.DMA((3,))] * 4,
        compiler_params=pltpu.CompilerParams(
            vmem_limit_bytes=50 << 20, collective_id=0, has_side_effects=True
        ),
        name="reciprocal",
    )(grid, keep, turn, *[jnp.asarray(t) for t in tables()])
    out_own, out_before = pl.pallas_call(
        sample_kernel,
        out_shape=[jax.ShapeDtypeStruct((3, ATOM_DEV), f32)] * 2,
        in_specs=[VM] * 3,
        out_specs=[VM] * 2,
        scratch_shapes=[pltpu.VMEM((768, 768), bf16)],
        compiler_params=limit,
        name="sample",
    )(own, before, pot)
    direct = pl.pallas_call(
        direct_kernel,
        out_shape=jax.ShapeDtypeStruct((3, ATOM_DEV), f32),
        in_specs=[SM] * 3 + [VM] * 3,
        out_specs=VM,
        scratch_shapes=[pltpu.VMEM((48, 8, CL), f32), pltpu.VMEM((CLU_DEV, 8, CL), f32)],
        compiler_params=limit,
        name="direct",
    )(pair_home, pair_other, pair_count, own, before, jnp.concatenate([after, after[:2]], 0))
    return direct + out_own + lax.ppermute(out_before, AXES, down)


def solution(mesh):
    placed = (
        P(None, AXES),
        P(None, AXES),
        P(None, None, AXES),
        P(None, None, AXES),
        P(AXES),
        P(AXES),
        P(AXES),
        P(AXES),
        P(AXES),
        P(AXES),
        P(None, AXES, None),
    )
    return jax.shard_map(
        on_device, mesh=mesh, in_specs=placed, out_specs=P(None, AXES), check_vma=False
    )
```

```python
import functools

import jax
import jax.numpy as jnp
import numpy as np
from jax import lax
from jax.experimental import pallas as pl
from jax.experimental.pallas import tpu as pltpu
from jax.sharding import PartitionSpec as P

CL = 128
CLU_DEV = 16
GX = 384
GY = 256
GZ = 256
DEV = 128
ATOM_DEV = 2048
SLOTS = 32
CHUNK = 512
AXES = ("grp", "sp")

f32, bf16 = jnp.float32, jnp.bfloat16
VM = pl.BlockSpec(memory_space=pltpu.VMEM)
SM = pl.BlockSpec(memory_space=pltpu.SMEM)


def halves(table):
    high = table.astype(bf16)
    low = (table - high.astype(np.float64)).astype(bf16)
    return high, low


@functools.cache
def tables():
    t = np.arange(128)[:, None]
    d = np.where(t < 64, 2 * t, 255 - 2 * t)
    y = np.arange(GY)[None, :]
    angle = 2 * np.pi * ((d * y) % GY) / GY
    real, imag = np.cos(angle), -np.sin(angle)
    imag[0] = 1 - 2 * (np.arange(GY) % 2)
    forward_y = np.concatenate([real, imag], 0)
    scale = np.full((1, 256), 2.0)
    scale[0, 0] = scale[0, 128] = 1.0
    backward_y = forward_y.T * scale / (GX * GY * GZ)
    z = np.arange(GZ)
    angle = 2 * np.pi * ((z[:, None] * z[None, :]) % GZ) / GZ
    cos, sin = np.cos(angle), np.sin(angle)
    forward_z = np.block([[cos, -sin], [sin, cos]])
    backward_z = np.block([[cos, sin], [-sin, cos]])
    k = np.arange(GX)
    forward_x = []
    for p in range(3):
        angle = 2 * np.pi * ((k[:, None] * (3 * np.arange(128)[None, :] + p)) % GX) / GX
        forward_x += [np.cos(angle), np.sin(angle)]
    backward_x = np.concatenate(
        [np.concatenate([forward_x[2 * p].T, forward_x[2 * p + 1].T], 1) for p in range(3)], 0
    )
    forward_x = np.concatenate(forward_x, 1)
    flip_x = np.eye(GX)[:, -np.arange(GX) % GX]
    flip_z = np.eye(GZ)[:, -np.arange(GZ) % GZ]
    out = [flip_x.astype(bf16), flip_z.astype(bf16)]
    for table in (forward_y, forward_x, forward_z, backward_z, backward_x, backward_y):
        out += list(halves(table))
    return out


def split(x):
    high = x.astype(bf16)
    return high, (x - high.astype(f32)).astype(bf16)


def nn(a, b):
    return lax.dot_general(a, b, (((1,), (0,)), ((), ())), preferred_element_type=f32)


def nt(a, b):
    return lax.dot_general(a, b, (((1,), (1,)), ((), ())), preferred_element_type=f32)


def left(table_high, table_low, x):
    high, low = split(x)
    return nn(
        jnp.concatenate([table_high, table_high, table_low], 1),
        jnp.concatenate([high, low, high], 0),
    )


def right(x, table_high, table_low):
    high, low = split(x)
    return nn(
        jnp.concatenate([high, low, high], 1),
        jnp.concatenate([table_high, table_high, table_low], 0),
    )


def step_masks(base, n, kind):
    it = lax.broadcasted_iota(jnp.int32, (256, n), 0)
    at = [(base + k) & 255 for k in range(4)]
    if kind == bf16:
        it = it.astype(f32).astype(bf16)
        at = [x.astype(f32).astype(bf16) for x in at]
    return [it == x for x in at]


def pick(masks, w):
    r = jnp.where(masks[3], w[3], jnp.zeros((), w[0].dtype))
    for k in (2, 1, 0):
        r = jnp.where(masks[k], w[k], r)
    return r


def split_list(w):
    high = [x.astype(bf16) for x in w]
    return high, [(x - y.astype(f32)).astype(bf16) for x, y in zip(w, high)]


def plane_weights(local, w, step):
    step = step - local
    r = jnp.zeros_like(w[0])
    for k in range(4):
        r = jnp.where(step == k, w[k], r)
    return r


class Atoms:
    def __init__(self, shift, first, dipoles, values, slopes, plane, row, column):
        self.shift, self.first = shift, first
        self.refs = (dipoles, values, slopes, plane, row, column)

    def read(self, start):
        cols = pl.ds(pl.multiple_of(start, CHUNK), CHUNK)
        dipoles, values, slopes, plane, row, column = self.refs
        m = [dipoles[a : a + 1, cols] for a in range(3)]
        v = [[values[a, k : k + 1, cols] for k in range(4)] for a in range(3)]
        s = [[slopes[a, k : k + 1, cols] for k in range(4)] for a in range(3)]
        return row[:, cols], column[:, cols], plane[:, cols] - self.first, m, v, s


def spread_chunk(cell, start, planes, grid):
    row, column, local, m, v, s = cell.read(start)
    at_z = step_masks(column, CHUNK, bf16)
    vh, vl = [pick(at_z, w) for w in split_list(v[2])]
    sh, sl = [pick(at_z, w) for w in split_list(s[2])]
    right_side = jnp.concatenate([vh, sh, vl, vh, sl, sh], 1)
    at_y = step_masks(row, CHUNK, bf16)
    for p in planes:
        x0 = plane_weights(local, v[0], p + cell.shift)
        xs = plane_weights(local, s[0], p + cell.shift)
        a, b, c = m[0] * xs, m[1] * x0, m[2] * x0
        w1 = [a * v[1][k] + b * s[1][k] for k in range(4)]
        w2 = [c * v[1][k] for k in range(4)]
        ah, al = [pick(at_y, w) for w in split_list(w1)]
        bh, bl = [pick(at_y, w) for w in split_list(w2)]
        grid[p * 256 : p * 256 + 256, :] += nt(
            jnp.concatenate([ah, bh, ah, al, bh, bl], 1), right_side
        )


def sample_chunk(cell, start, p, stacked, out):
    row, column, local, m, v, s = cell.read(start)
    at_z = step_masks(column, CHUNK, bf16)
    vh, vl = [pick(at_z, w) for w in split_list(v[2])]
    sh, sl = [pick(at_z, w) for w in split_list(s[2])]
    at_y = step_masks(row, CHUNK, f32)
    v1, s1 = pick(at_y, v[1]), pick(at_y, s[1])
    x0 = plane_weights(local, v[0], p + cell.shift)
    xs = plane_weights(local, s[0], p + cell.shift)
    tv = nn(stacked, jnp.concatenate([vh, vl, vh], 0))
    ts = nn(stacked, jnp.concatenate([sh, sl, sh], 0))
    r = [
        xs * jnp.sum(v1 * tv, 0, keepdims=True),
        x0 * jnp.sum(s1 * tv, 0, keepdims=True),
        x0 * jnp.sum(v1 * ts, 0, keepdims=True),
    ]
    out[:, pl.ds(pl.multiple_of(start, CHUNK), CHUNK)] -= jnp.concatenate(r, 0)


def extend(parts, ext):
    for part, (positions, dipoles) in enumerate(parts):
        for c in range(CLU_DEV):
            cols = slice(c * CL, c * CL + CL)
            x = positions[:, cols]
            if part != 1:
                shift = 2.0 * (part - 1)
                x = x + jnp.where(lax.broadcasted_iota(jnp.int32, (3, CL), 0) == 0, shift, 0.0)
            ext[part * CLU_DEV + c, 0:3, :] = x
            ext[part * CLU_DEV + c, 3:6, :] = dipoles[:, cols]


def direct_slots(lo, hi, home, other, count, ext, acc):
    eye = (
        lax.broadcasted_iota(jnp.int32, (CL, CL), 0) == lax.broadcasted_iota(jnp.int32, (CL, CL), 1)
    ).astype(f32)
    which = lax.broadcasted_iota(jnp.int32, (CLU_DEV, 8, CL), 0)

    def slot(t, carry):
        h, o = home[t], other[t]
        hx = ext[h + CLU_DEV]
        ox = ext[o].T
        delta = [hx[a : a + 1, :] - ox[:, a : a + 1] for a in range(3)]
        m = [ox[:, 3 + a : 4 + a] for a in range(3)]
        q = delta[0] * delta[0] + delta[1] * delta[1] + delta[2] * delta[2]
        inverse = lax.rsqrt(q + 0.25)
        square = inverse * inverse
        self_slot = jnp.where(o == h + CLU_DEV, 1.0, 0.0)
        first = jnp.exp(-0.5 * q) * (inverse * square) * (1.0 - self_slot * eye)
        second = 3.0 * first * square
        along = second * (delta[0] * m[0] + delta[1] * m[1] + delta[2] * m[2])
        e = [jnp.sum(along * delta[a] - first * m[a], 0, keepdims=True) for a in range(3)]
        live = jnp.where(t < count[0], 0.125, 0.0)
        e = jnp.concatenate(e + [jnp.zeros((5, CL), f32)], 0) * live
        acc[...] += jnp.where(which == h, e[None], 0.0)
        return carry

    lax.fori_loop(lo, hi, slot, 0, unroll=4)


def device_id(t):
    return (t // 64, lax.rem(t, 64))


def remote(src, dst, send_sem, recv_sem, t):
    return pltpu.make_async_remote_copy(
        src_ref=src,
        dst_ref=dst,
        send_sem=send_sem,
        recv_sem=recv_sem,
        device_id=device_id(t),
        device_id_type=pl.DeviceIdType.MESH,
    )


def exchange_start(me, p, src, dst, send_sem, recv_sem):
    def send(i, c):
        t = lax.rem(me + i, DEV)
        remote(src.at[p, t], dst.at[p, me], send_sem.at[p], recv_sem.at[p], t).start()
        return c

    lax.fori_loop(1, DEV, send, 0)
    dst[p, pl.ds(me, 1)] = src[p, pl.ds(me, 1)]


def exchange_wait(p, src, sem):
    part = src.at[p, pl.ds(0, DEV - 1)]
    pltpu.make_async_copy(part, part, sem.at[p]).wait()


def to_rows(ref, p, value):
    view = ref.at[p].reshape(512, 128)
    for c in range(2):
        for h in range(2):
            view[pl.ds(2 * c + h, 128, stride=4), :] = value[
                c * 128 : c * 128 + 128, h * 128 : h * 128 + 128
            ]


def from_rows(ref, p):
    view = ref.at[p].reshape(512, 128)
    part = [view[pl.ds(k, 128, stride=4), :] for k in range(4)]
    return jnp.concatenate(part[0:2], 1), jnp.concatenate(part[2:4], 1)


def flipped(x, flip_x, flip_z):
    high, low = split(x)
    y = nn(flip_x, jnp.concatenate([high, low], 1))
    high, low = split(y[:, 0:GZ] + y[:, GZ:])
    y = nn(jnp.concatenate([high, low], 0), flip_z)
    return y[0:GX] + y[GX:]


N_TABLES = 14
N_ATOM = 7


def kernel(*refs):
    refs = list(refs)
    take = lambda n: [refs.pop(0) for _ in range(n)]
    home, other, count = take(3)
    own_refs = take(N_ATOM)
    influence, *table_hbm = take(1 + N_TABLES)
    (out,) = take(1)
    before_refs = take(N_ATOM)
    after_refs = take(2)
    table = take(N_TABLES)
    rows_in, sent, got, keep, turn = take(5)
    send1, recv1, send2, recv2, spec, other_spec, grid, ext, acc, out_before, returned = take(11)
    ss1, rs1, ss2, rs2, atom_ss, atom_rs, table_sem, rows_sem, infl_sem, back_sem = take(10)

    me = lax.axis_index("grp") * 64 + lax.axis_index("sp")
    above, below = lax.rem(me + 1, DEV), lax.rem(me + DEV - 1, DEV)
    loads = [
        pltpu.make_async_copy(a, b, table_sem.at[i])
        for i, (a, b) in enumerate(zip(table_hbm, table))
    ]
    rows_load = pltpu.make_async_copy(influence, rows_in, rows_sem)
    rows_load.start()
    for load in loads:
        load.start()
    barrier = pltpu.get_barrier_semaphore()

    def greet(i, c):
        pl.semaphore_signal(
            barrier,
            inc=1,
            device_id=device_id(lax.rem(me + i, DEV)),
            device_id_type=pl.DeviceIdType.MESH,
        )
        return c

    lax.fori_loop(1, DEV, greet, 0)
    own = Atoms(0, 3 * me, *own_refs[1:])
    before = Atoms(3, 3 * below, *before_refs[1:])
    chunks = ATOM_DEV // CHUNK

    def loop(lo, hi, f):
        def step(i, c):
            f(i * CHUNK)
            return c

        lax.fori_loop(lo, hi, step, 0)

    grid[...] = jnp.zeros_like(grid)
    out[...] = jnp.zeros_like(out)
    out_before[...] = jnp.zeros_like(out_before)
    acc[...] = jnp.zeros_like(acc)
    ext[...] = jnp.zeros_like(ext)
    loop(0, 2, lambda start: spread_chunk(own, start, range(3), grid))

    pl.semaphore_wait(barrier, DEV - 1)
    copies = [
        remote(a, b, atom_ss.at[i], atom_rs.at[i], above)
        for i, (a, b) in enumerate(zip(own_refs, before_refs))
    ]
    copies += [
        remote(a, b, atom_ss.at[N_ATOM + i], atom_rs.at[N_ATOM + i], below)
        for i, (a, b) in enumerate(zip(own_refs[:2], after_refs))
    ]
    for copy in copies:
        copy.start()
    rows_load.wait()
    lower = me < 64
    sent[...] = jnp.where(lower, rows_in[:, 1, :], rows_in[:, 0, :])
    target = jnp.where(lower, 127 - me, lax.rem(DEV - me, 64))
    infl_copy = remote(sent, got, infl_sem.at[0], infl_sem.at[1], target)
    infl_copy.start()

    loop(2, chunks, lambda start: spread_chunk(own, start, range(3), grid))
    for copy in copies:
        copy.wait()
    for load in loads:
        load.wait()
    flip_x, flip_z, fyh, fyl, fxh, fxl, fzh, fzl, bzh, bzl, bxh, bxl, byh, byl = table
    for p in range(3):
        loop(0, chunks, lambda start: spread_chunk(before, start, (p,), grid))
        to_rows(send1, p, left(fyh[...], fyl[...], grid[p * 256 : p * 256 + 256, :]))
        exchange_start(me, p, send1, recv1, ss1, rs1)

    extend(
        ((before_refs[0], before_refs[1]), (own_refs[0], own_refs[1]), (after_refs[0], after_refs[1])), ext
    )
    direct_slots(0, SLOTS // 2, home, other, count, ext, acc)
    infl_copy.wait()
    kept = jnp.where(lower, rows_in[:, 0, :], rows_in[:, 1, :])
    u, v = jnp.where(lower, kept, got[...]), jnp.where(lower, got[...], kept)
    same, turned = 0.5 * u, 0.5 * v
    both = 0.25 * (u + v)
    first = me == 0
    keep[...] = jnp.where(first, both, same) + flipped(
        jnp.where(first, both, turned), flip_x[...], flip_z[...]
    )

    @pl.when(first)
    def _():
        q = 0.25 * (rows_in[:, 0, :] - got[...])
        turn[...] = q + flipped(q, flip_x[...], flip_z[...])

    for p in range(3):
        exchange_wait(p, recv1, rs1)
        cols = slice(p * 256, p * 256 + 256)

        def stage(sign):
            real, imag = from_rows(recv1, p)
            imag = imag * sign
            x = jnp.concatenate(
                [jnp.concatenate([real, imag], 1), jnp.concatenate([imag, -real], 1)], 0
            )
            return left(fxh[:, cols], fxl[:, cols], x)

        if p == 0:
            spec[...] = stage(1.0)
        else:
            spec[...] += stage(1.0)

        @pl.when(first)
        def _():
            if p == 0:
                other_spec[...] = stage(-1.0)
            else:
                other_spec[...] += stage(-1.0)

    twice = lambda x: jnp.concatenate([x, x], 1)
    spec[...] = right(spec[...], fzh[...], fzl[...]) * twice(keep[...])

    @pl.when(first)
    def _():
        spec[...] += right(other_spec[...], fzh[...], fzl[...]) * twice(turn[...])

    back = right(spec[...], bzh[...], bzl[...])
    real, imag = back[:, 0:256], back[:, 256:512]
    x = jnp.concatenate([jnp.concatenate([real, imag], 1), jnp.concatenate([-imag, real], 1)], 0)
    high, low = split(x)
    x = jnp.concatenate([high, low, high], 0)
    for p in range(3):
        rows = slice(p * 128, p * 128 + 128)
        y = nn(jnp.concatenate([bxh[rows, :], bxh[rows, :], bxl[rows, :]], 1), x)
        to_rows(send2, p, jnp.concatenate([y[:, 0:256], y[:, 256:512]], 0))
        exchange_start(me, p, send2, recv2, ss2, rs2)

    direct_slots(SLOTS // 2, SLOTS, home, other, count, ext, acc)
    back_copy = remote(out_before, returned, back_sem.at[0], back_sem.at[1], below)
    for p in range(3):
        exchange_wait(p, recv2, rs2)
        real, imag = from_rows(recv2, p)
        high, low = split(left(byh[...], byl[...], jnp.concatenate([real, imag], 0)))
        stacked = jnp.concatenate([high, high, low], 1)
        loop(0, chunks, lambda start: sample_chunk(before, start, p, stacked, out_before))
        if p == 2:
            back_copy.start()
        loop(0, chunks, lambda start: sample_chunk(own, start, p, stacked, out))
    back_copy.wait()
    for c in range(CLU_DEV):
        cols = slice(c * CL, c * CL + CL)
        out[:, cols] += returned[:, cols] + acc[c, 0:3, :]
    for p in range(3):
        exchange_wait(p, send1, ss1)
        exchange_wait(p, send2, ss2)


def on_device(
    positions,
    dipoles,
    spline_values,
    spline_slopes,
    plane_base,
    row_base,
    column_base,
    pair_home,
    pair_other,
    pair_count,
    influence,
):
    constants = [jnp.asarray(t) for t in tables()]
    own = [
        positions,
        dipoles,
        spline_values,
        spline_slopes,
        plane_base.reshape(1, ATOM_DEV),
        row_base.reshape(1, ATOM_DEV),
        column_base.reshape(1, ATOM_DEV),
    ]
    vm = lambda x: pltpu.VMEM(x.shape, x.dtype)
    blocks = pltpu.VMEM((3, DEV, 4, 128), f32)
    return pl.pallas_call(
        kernel,
        out_shape=jax.ShapeDtypeStruct((3, ATOM_DEV), f32),
        in_specs=[SM] * 3 + [VM] * N_ATOM + [pl.BlockSpec(memory_space=pltpu.HBM)] * (1 + N_TABLES),
        out_specs=VM,
        scratch_shapes=[vm(x) for x in own]
        + [vm(x) for x in own[:2]]
        + [vm(x) for x in constants]
        + [pltpu.VMEM((GX, 2, GZ), f32)]
        + [pltpu.VMEM((GX, GZ), f32)] * 4
        + [blocks] * 4
        + [pltpu.VMEM((GX, 512), f32)] * 2
        + [
            pltpu.VMEM((768, 256), f32),
            pltpu.VMEM((48, 8, CL), f32),
            pltpu.VMEM((CLU_DEV, 8, CL), f32),
            pltpu.VMEM((3, ATOM_DEV), f32),
            pltpu.VMEM((3, ATOM_DEV), f32),
        ]
        + [pltpu.SemaphoreType.DMA((3,))] * 4
        + [pltpu.SemaphoreType.DMA((N_ATOM + 2,))] * 2
        + [pltpu.SemaphoreType.DMA((N_TABLES,)), pltpu.SemaphoreType.DMA]
        + [pltpu.SemaphoreType.DMA((2,))] * 2,
        compiler_params=pltpu.CompilerParams(
            vmem_limit_bytes=62 << 20, collective_id=0, has_side_effects=True
        ),
        name="polarization",
    )(pair_home, pair_other, pair_count, *own, influence, *constants)


def solution(mesh):
    placed = (
        P(None, AXES),
        P(None, AXES),
        P(None, None, AXES),
        P(None, None, AXES),
        P(AXES),
        P(AXES),
        P(AXES),
        P(AXES),
        P(AXES),
        P(AXES),
        P(None, AXES, None),
    )
    return jax.shard_map(
        on_device, mesh=mesh, in_specs=placed, out_specs=P(None, AXES), check_vma=False
    )
```

```python
import functools

import jax
import jax.numpy as jnp
import numpy as np
from jax import lax
from jax.experimental import pallas as pl
from jax.experimental.pallas import tpu as pltpu
from jax.sharding import PartitionSpec as P

CL = 128
CLU_DEV = 16
GX = 384
GY = 256
GZ = 256
DEV = 128
ATOM_DEV = 2048
SLOTS = 32
CHUNK = 512
AXES = ("grp", "sp")

f32, bf16 = jnp.float32, jnp.bfloat16
VM = pl.BlockSpec(memory_space=pltpu.VMEM)
SM = pl.BlockSpec(memory_space=pltpu.SMEM)


def halves(table):
    high = table.astype(bf16)
    low = (table - high.astype(np.float64)).astype(bf16)
    return high, low


@functools.cache
def tables():
    t = np.arange(128)[:, None]
    d = np.where(t < 64, 2 * t, 255 - 2 * t)
    y = np.arange(GY)[None, :]
    angle = 2 * np.pi * ((d * y) % GY) / GY
    real, imag = np.cos(angle), -np.sin(angle)
    imag[0] = 1 - 2 * (np.arange(GY) % 2)
    forward_y = np.concatenate([real, imag], 0)
    scale = np.full((1, 256), 2.0)
    scale[0, 0] = scale[0, 128] = 1.0
    backward_y = forward_y.T * scale / (GX * GY * GZ)
    z = np.arange(GZ)
    angle = 2 * np.pi * ((z[:, None] * z[None, :]) % GZ) / GZ
    cos, sin = np.cos(angle), np.sin(angle)
    forward_z = np.block([[cos, -sin], [sin, cos]])
    backward_z = np.block([[cos, sin], [-sin, cos]])
    k = np.arange(GX)
    forward_x = []
    for p in range(3):
        angle = 2 * np.pi * ((k[:, None] * (3 * np.arange(128)[None, :] + p)) % GX) / GX
        forward_x += [np.cos(angle), np.sin(angle)]
    backward_x = np.concatenate(
        [np.concatenate([forward_x[2 * p].T, forward_x[2 * p + 1].T], 1) for p in range(3)], 0
    )
    forward_x = np.concatenate(forward_x, 1)
    flip_x = np.eye(GX)[:, -np.arange(GX) % GX]
    flip_z = np.eye(GZ)[:, -np.arange(GZ) % GZ]
    out = [flip_x.astype(bf16), flip_z.astype(bf16)]
    for table in (forward_y, forward_x, forward_z, backward_z, backward_x, backward_y):
        out += list(halves(table))
    return out


def split(x):
    high = x.astype(bf16)
    return high, (x - high.astype(f32)).astype(bf16)


def nn(a, b):
    return lax.dot_general(a, b, (((1,), (0,)), ((), ())), preferred_element_type=f32)


def nt(a, b):
    return lax.dot_general(a, b, (((1,), (1,)), ((), ())), preferred_element_type=f32)


def left(table_high, table_low, x):
    high, low = split(x)
    return nn(
        jnp.concatenate([table_high, table_high, table_low], 1),
        jnp.concatenate([high, low, high], 0),
    )


def right(x, table_high, table_low):
    high, low = split(x)
    return nn(
        jnp.concatenate([high, low, high], 1),
        jnp.concatenate([table_high, table_high, table_low], 0),
    )


def step_masks(base, n, kind):
    it = lax.broadcasted_iota(jnp.int32, (256, n), 0)
    at = [(base + k) & 255 for k in range(4)]
    if kind == bf16:
        it = it.astype(f32).astype(bf16)
        at = [x.astype(f32).astype(bf16) for x in at]
    return [it == x for x in at]


def pick(masks, w):
    r = jnp.where(masks[3], w[3], jnp.zeros((), w[0].dtype))
    for k in (2, 1, 0):
        r = jnp.where(masks[k], w[k], r)
    return r


def split_list(w):
    high = [x.astype(bf16) for x in w]
    return high, [(x - y.astype(f32)).astype(bf16) for x, y in zip(w, high)]


def plane_weights(local, w, step):
    step = step - local
    r = jnp.zeros_like(w[0])
    for k in range(4):
        r = jnp.where(step == k, w[k], r)
    return r


class Atoms:
    def __init__(self, shift, first, dipoles, values, slopes, plane, row, column):
        self.shift, self.first = shift, first
        self.refs = (dipoles, values, slopes, plane, row, column)

    def read(self, start):
        cols = pl.ds(pl.multiple_of(start, CHUNK), CHUNK)
        dipoles, values, slopes, plane, row, column = self.refs
        m = [dipoles[a : a + 1, cols] for a in range(3)]
        v = [[values[a, k : k + 1, cols] for k in range(4)] for a in range(3)]
        s = [[slopes[a, k : k + 1, cols] for k in range(4)] for a in range(3)]
        return row[:, cols], column[:, cols], plane[:, cols] - self.first, m, v, s


def spread_chunk(cell, start, planes, grid, zt):
    row, column, local, m, v, s = cell.read(start)
    at_z = step_masks(column, CHUNK, bf16)
    vh, vl = [pick(at_z, w) for w in split_list(v[2])]
    sh, sl = [pick(at_z, w) for w in split_list(s[2])]
    cols = pl.ds(pl.multiple_of(start, CHUNK), CHUNK)
    for k, x in enumerate((vh, vl, sh, sl)):
        zt[k, :, cols] = x
    right_side = jnp.concatenate([vh, sh, vl, vh, sl, sh], 1)
    at_y = step_masks(row, CHUNK, bf16)
    for p in planes:
        x0 = plane_weights(local, v[0], p + cell.shift)
        xs = plane_weights(local, s[0], p + cell.shift)
        a, b, c = m[0] * xs, m[1] * x0, m[2] * x0
        w1 = [a * v[1][k] + b * s[1][k] for k in range(4)]
        w2 = [c * v[1][k] for k in range(4)]
        ah, al = [pick(at_y, w) for w in split_list(w1)]
        bh, bl = [pick(at_y, w) for w in split_list(w2)]
        grid[p * 256 : p * 256 + 256, :] += nt(
            jnp.concatenate([ah, bh, ah, al, bh, bl], 1), right_side
        )


def row_tables(cell, start, yt):
    row, column, local, m, v, s = cell.read(start)
    at_y = step_masks(row, CHUNK, f32)
    cols = pl.ds(pl.multiple_of(start, CHUNK), CHUNK)
    yt[0, :, cols] = pick(at_y, v[1])
    yt[1, :, cols] = pick(at_y, s[1])


def sample_chunk(cell, start, stacked, zt, yt, out):
    row, column, local, m, v, s = cell.read(start)
    cols = pl.ds(pl.multiple_of(start, CHUNK), CHUNK)
    vh, vl, sh, sl = [zt[k, :, cols] for k in range(4)]
    v_side, s_side = jnp.concatenate([vh, vl, vh], 0), jnp.concatenate([sh, sl, sh], 0)
    v1, s1 = yt[0, :, cols], yt[1, :, cols]
    total = jnp.zeros((3, CHUNK), f32)
    for p in range(3):
        x0 = plane_weights(local, v[0], p + cell.shift)
        xs = plane_weights(local, s[0], p + cell.shift)
        pot = stacked[p * 256 : p * 256 + 256, :]
        tv, ts = nn(pot, v_side), nn(pot, s_side)
        r = [
            xs * jnp.sum(v1 * tv, 0, keepdims=True),
            x0 * jnp.sum(s1 * tv, 0, keepdims=True),
            x0 * jnp.sum(v1 * ts, 0, keepdims=True),
        ]
        total = total + jnp.concatenate(r, 0)
    out[:, cols] = -total


def extend(parts, ext):
    for part, (positions, dipoles) in enumerate(parts):
        for c in range(CLU_DEV):
            cols = slice(c * CL, c * CL + CL)
            x = positions[:, cols]
            if part != 1:
                shift = 2.0 * (part - 1)
                x = x + jnp.where(lax.broadcasted_iota(jnp.int32, (3, CL), 0) == 0, shift, 0.0)
            ext[part * CLU_DEV + c, 0:3, :] = x
            ext[part * CLU_DEV + c, 3:6, :] = dipoles[:, cols]


def direct_slots(lo, hi, home, other, count, ext, acc):
    eye = (
        lax.broadcasted_iota(jnp.int32, (CL, CL), 0) == lax.broadcasted_iota(jnp.int32, (CL, CL), 1)
    ).astype(f32)
    which = lax.broadcasted_iota(jnp.int32, (CLU_DEV, 8, CL), 0)

    def slot(t, carry):
        h, o = home[t], other[t]
        hx = ext[h + CLU_DEV]
        ox = ext[o].T
        delta = [hx[a : a + 1, :] - ox[:, a : a + 1] for a in range(3)]
        m = [ox[:, 3 + a : 4 + a] for a in range(3)]
        q = delta[0] * delta[0] + delta[1] * delta[1] + delta[2] * delta[2]
        inverse = lax.rsqrt(q + 0.25)
        square = inverse * inverse
        self_slot = jnp.where(o == h + CLU_DEV, 1.0, 0.0)
        first = jnp.exp(-0.5 * q) * (inverse * square) * (1.0 - self_slot * eye)
        second = 3.0 * first * square
        along = second * (delta[0] * m[0] + delta[1] * m[1] + delta[2] * m[2])
        e = [jnp.sum(along * delta[a] - first * m[a], 0, keepdims=True) for a in range(3)]
        live = jnp.where(t < count[0], 0.125, 0.0)
        e = jnp.concatenate(e + [jnp.zeros((5, CL), f32)], 0) * live
        acc[...] += jnp.where(which == h, e[None], 0.0)
        return carry

    lax.fori_loop(lo, hi, slot, 0, unroll=4)


def device_id(t):
    return (t >> 6, t & 63)


def remote(src, dst, send_sem, recv_sem, t):
    return pltpu.make_async_remote_copy(
        src_ref=src,
        dst_ref=dst,
        send_sem=send_sem,
        recv_sem=recv_sem,
        device_id=device_id(t),
        device_id_type=pl.DeviceIdType.MESH,
    )


def exchange_start(me, p, src, dst, send_sem, recv_sem):
    def send(i, c):
        t = (me + i) & (DEV - 1)
        remote(src.at[p, t], dst.at[p, me], send_sem.at[p], recv_sem.at[p], t).start()
        return c

    lax.fori_loop(1, DEV, send, 0, unroll=8)
    dst[p, pl.ds(me, 1)] = src[p, pl.ds(me, 1)]


def exchange_wait(p, src, sem):
    part = src.at[p, pl.ds(0, DEV - 1)]
    pltpu.make_async_copy(part, part, sem.at[p]).wait()


def to_rows(ref, p, value):
    view = ref.at[p].reshape(512, 128)
    for c in range(2):
        for h in range(2):
            view[pl.ds(2 * c + h, 128, stride=4), :] = value[
                c * 128 : c * 128 + 128, h * 128 : h * 128 + 128
            ]


def from_rows(ref, p):
    view = ref.at[p].reshape(512, 128)
    part = [view[pl.ds(k, 128, stride=4), :] for k in range(4)]
    return jnp.concatenate(part[0:2], 1), jnp.concatenate(part[2:4], 1)


def flipped(x, flip_x, flip_z):
    high, low = split(x)
    y = nn(flip_x, jnp.concatenate([high, low], 1))
    high, low = split(y[:, 0:GZ] + y[:, GZ:])
    y = nn(jnp.concatenate([high, low], 0), flip_z)
    return y[0:GX] + y[GX:]


N_TABLES = 14
N_ATOM = 7


def kernel(*refs):
    refs = list(refs)
    take = lambda n: [refs.pop(0) for _ in range(n)]
    home, other, count = take(3)
    own_refs = take(N_ATOM)
    influence, *table_hbm = take(1 + N_TABLES)
    (out,) = take(1)
    before_refs = take(N_ATOM)
    after_refs = take(2)
    table = take(N_TABLES)
    rows_in, sent, got, keep, turn = take(5)
    send1, recv1, send2, recv2, spec, other_spec, grid, ext, acc, out_before, returned = take(11)
    own_zt, before_zt, own_yt, before_yt, stacked = take(5)
    ss1, rs1, ss2, rs2, atom_ss, atom_rs, table_sem, rows_sem, infl_sem, back_sem = take(10)

    me = lax.axis_index("grp") * 64 + lax.axis_index("sp")
    above, below = lax.rem(me + 1, DEV), lax.rem(me + DEV - 1, DEV)
    loads = [
        pltpu.make_async_copy(a, b, table_sem.at[i])
        for i, (a, b) in enumerate(zip(table_hbm, table))
    ]
    rows_load = pltpu.make_async_copy(influence, rows_in, rows_sem)
    rows_load.start()
    for load in loads:
        load.start()
    barrier = pltpu.get_barrier_semaphore()

    def greet(i, c):
        pl.semaphore_signal(
            barrier,
            inc=1,
            device_id=device_id((me + i) & (DEV - 1)),
            device_id_type=pl.DeviceIdType.MESH,
        )
        return c

    lax.fori_loop(1, DEV, greet, 0, unroll=4)
    own = Atoms(0, 3 * me, *own_refs[1:])
    before = Atoms(3, 3 * below, *before_refs[1:])
    chunks = ATOM_DEV // CHUNK

    def loop(lo, hi, f):
        def step(i, c):
            f(i * CHUNK)
            return c

        lax.fori_loop(lo, hi, step, 0)

    grid[...] = jnp.zeros_like(grid)
    acc[...] = jnp.zeros_like(acc)
    ext[...] = jnp.zeros_like(ext)
    loop(0, 2, lambda start: spread_chunk(own, start, range(3), grid, own_zt))

    pl.semaphore_wait(barrier, DEV - 1)
    copies = [
        remote(a, b, atom_ss.at[i], atom_rs.at[i], above)
        for i, (a, b) in enumerate(zip(own_refs, before_refs))
    ]
    copies += [
        remote(a, b, atom_ss.at[N_ATOM + i], atom_rs.at[N_ATOM + i], below)
        for i, (a, b) in enumerate(zip(own_refs[:2], after_refs))
    ]
    for copy in copies:
        copy.start()
    rows_load.wait()
    lower = me < 64
    sent[...] = jnp.where(lower, rows_in[:, 1, :], rows_in[:, 0, :])
    target = jnp.where(lower, 127 - me, lax.rem(DEV - me, 64))
    infl_copy = remote(sent, got, infl_sem.at[0], infl_sem.at[1], target)
    infl_copy.start()

    loop(2, chunks, lambda start: spread_chunk(own, start, range(3), grid, own_zt))
    for copy in copies:
        copy.wait()
    for load in loads:
        load.wait()
    flip_x, flip_z, fyh, fyl, fxh, fxl, fzh, fzl, bzh, bzl, bxh, bxl, byh, byl = table
    loop(0, chunks, lambda start: spread_chunk(before, start, range(3), grid, before_zt))
    for p in range(3):
        to_rows(send1, p, left(fyh[...], fyl[...], grid[p * 256 : p * 256 + 256, :]))
        exchange_start(me, p, send1, recv1, ss1, rs1)

    extend(
        ((before_refs[0], before_refs[1]), (own_refs[0], own_refs[1]), (after_refs[0], after_refs[1])), ext
    )
    direct_slots(0, SLOTS // 2, home, other, count, ext, acc)
    infl_copy.wait()
    kept = jnp.where(lower, rows_in[:, 0, :], rows_in[:, 1, :])
    u, v = jnp.where(lower, kept, got[...]), jnp.where(lower, got[...], kept)
    same, turned = 0.5 * u, 0.5 * v
    both = 0.25 * (u + v)
    first = me == 0
    keep[...] = jnp.where(first, both, same) + flipped(
        jnp.where(first, both, turned), flip_x[...], flip_z[...]
    )

    @pl.when(first)
    def _():
        q = 0.25 * (rows_in[:, 0, :] - got[...])
        turn[...] = q + flipped(q, flip_x[...], flip_z[...])

    for p in range(3):
        exchange_wait(p, recv1, rs1)
        cols = slice(p * 256, p * 256 + 256)

        def stage(sign):
            real, imag = from_rows(recv1, p)
            imag = imag * sign
            x = jnp.concatenate(
                [jnp.concatenate([real, imag], 1), jnp.concatenate([imag, -real], 1)], 0
            )
            return left(fxh[:, cols], fxl[:, cols], x)

        if p == 0:
            spec[...] = stage(1.0)
        else:
            spec[...] += stage(1.0)

        @pl.when(first)
        def _():
            if p == 0:
                other_spec[...] = stage(-1.0)
            else:
                other_spec[...] += stage(-1.0)

    twice = lambda x: jnp.concatenate([x, x], 1)
    spec[...] = right(spec[...], fzh[...], fzl[...]) * twice(keep[...])

    @pl.when(first)
    def _():
        spec[...] += right(other_spec[...], fzh[...], fzl[...]) * twice(turn[...])

    back = right(spec[...], bzh[...], bzl[...])
    real, imag = back[:, 0:256], back[:, 256:512]
    x = jnp.concatenate([jnp.concatenate([real, imag], 1), jnp.concatenate([-imag, real], 1)], 0)
    high, low = split(x)
    x = jnp.concatenate([high, low, high], 0)
    for p in range(3):
        rows = slice(p * 128, p * 128 + 128)
        y = nn(jnp.concatenate([bxh[rows, :], bxh[rows, :], bxl[rows, :]], 1), x)
        to_rows(send2, p, jnp.concatenate([y[:, 0:256], y[:, 256:512]], 0))
        exchange_start(me, p, send2, recv2, ss2, rs2)

    direct_slots(SLOTS // 2, SLOTS, home, other, count, ext, acc)
    back_copy = remote(out_before, returned, back_sem.at[0], back_sem.at[1], below)
    loop(0, chunks, lambda start: row_tables(before, start, before_yt))
    loop(0, chunks, lambda start: row_tables(own, start, own_yt))
    for p in range(3):
        exchange_wait(p, recv2, rs2)
        real, imag = from_rows(recv2, p)
        high, low = split(left(byh[...], byl[...], jnp.concatenate([real, imag], 0)))
        stacked[p * 256 : p * 256 + 256, :] = jnp.concatenate([high, high, low], 1)
    loop(0, chunks, lambda start: sample_chunk(before, start, stacked, before_zt, before_yt, out_before))
    back_copy.start()
    loop(0, chunks, lambda start: sample_chunk(own, start, stacked, own_zt, own_yt, out))
    back_copy.wait()
    for c in range(CLU_DEV):
        cols = slice(c * CL, c * CL + CL)
        out[:, cols] += returned[:, cols] + acc[c, 0:3, :]
    for p in range(3):
        exchange_wait(p, send1, ss1)
        exchange_wait(p, send2, ss2)


def on_device(
    positions,
    dipoles,
    spline_values,
    spline_slopes,
    plane_base,
    row_base,
    column_base,
    pair_home,
    pair_other,
    pair_count,
    influence,
):
    constants = [jnp.asarray(t) for t in tables()]
    own = [
        positions,
        dipoles,
        spline_values,
        spline_slopes,
        plane_base.reshape(1, ATOM_DEV),
        row_base.reshape(1, ATOM_DEV),
        column_base.reshape(1, ATOM_DEV),
    ]
    vm = lambda x: pltpu.VMEM(x.shape, x.dtype)
    blocks = pltpu.VMEM((3, DEV, 4, 128), f32)
    return pl.pallas_call(
        kernel,
        out_shape=jax.ShapeDtypeStruct((3, ATOM_DEV), f32),
        in_specs=[SM] * 3 + [VM] * N_ATOM + [pl.BlockSpec(memory_space=pltpu.HBM)] * (1 + N_TABLES),
        out_specs=VM,
        scratch_shapes=[vm(x) for x in own]
        + [vm(x) for x in own[:2]]
        + [vm(x) for x in constants]
        + [pltpu.VMEM((GX, 2, GZ), f32)]
        + [pltpu.VMEM((GX, GZ), f32)] * 4
        + [blocks] * 4
        + [pltpu.VMEM((GX, 512), f32)] * 2
        + [
            pltpu.VMEM((768, 256), f32),
            pltpu.VMEM((48, 8, CL), f32),
            pltpu.VMEM((CLU_DEV, 8, CL), f32),
            pltpu.VMEM((3, ATOM_DEV), f32),
            pltpu.VMEM((3, ATOM_DEV), f32),
        ]
        + [pltpu.VMEM((4, 256, ATOM_DEV), bf16)] * 2
        + [pltpu.VMEM((2, 256, ATOM_DEV), f32)] * 2
        + [pltpu.VMEM((768, 768), bf16)]
        + [pltpu.SemaphoreType.DMA((3,))] * 4
        + [pltpu.SemaphoreType.DMA((N_ATOM + 2,))] * 2
        + [pltpu.SemaphoreType.DMA((N_TABLES,)), pltpu.SemaphoreType.DMA]
        + [pltpu.SemaphoreType.DMA((2,))] * 2,
        compiler_params=pltpu.CompilerParams(
            vmem_limit_bytes=62 << 20, collective_id=0, has_side_effects=True
        ),
        name="polarization",
    )(pair_home, pair_other, pair_count, *own, influence, *constants)


def solution(mesh):
    placed = (
        P(None, AXES),
        P(None, AXES),
        P(None, None, AXES),
        P(None, None, AXES),
        P(AXES),
        P(AXES),
        P(AXES),
        P(AXES),
        P(AXES),
        P(AXES),
        P(None, AXES, None),
    )
    return jax.shard_map(
        on_device, mesh=mesh, in_specs=placed, out_specs=P(None, AXES), check_vma=False
    )
```

```python
import functools

import jax
import jax.numpy as jnp
import numpy as np
from jax import lax
from jax.experimental import pallas as pl
from jax.experimental.pallas import tpu as pltpu
from jax.sharding import PartitionSpec as P

CL = 128
CLU_DEV = 16
GX = 384
GY = 256
GZ = 256
DEV = 128
ATOM_DEV = 2048
SLOTS = 32
CHUNK = 512
AXES = ("grp", "sp")

f32, bf16 = jnp.float32, jnp.bfloat16
VM = pl.BlockSpec(memory_space=pltpu.VMEM)
SM = pl.BlockSpec(memory_space=pltpu.SMEM)


def halves(table):
    high = table.astype(bf16)
    low = (table - high.astype(np.float64)).astype(bf16)
    return high, low


@functools.cache
def tables():
    t = np.arange(128)[:, None]
    d = np.where(t < 64, 2 * t, 255 - 2 * t)
    y = np.arange(GY)[None, :]
    angle = 2 * np.pi * ((d * y) % GY) / GY
    real, imag = np.cos(angle), -np.sin(angle)
    imag[0] = 1 - 2 * (np.arange(GY) % 2)
    forward_y = np.concatenate([real, imag], 0)
    scale = np.full((1, 256), 2.0)
    scale[0, 0] = scale[0, 128] = 1.0
    backward_y = forward_y.T * scale / (GX * GY * GZ)
    backward_y = np.concatenate([backward_y, backward_y[:16]], 0)
    z = np.arange(GZ)
    angle = 2 * np.pi * ((z[:, None] * z[None, :]) % GZ) / GZ
    cos, sin = np.cos(angle), np.sin(angle)
    order = 4 * (z % 64) + z // 64
    cos, sin = cos[order], sin[order]
    forward_z = np.block([[cos, -sin], [sin, cos]])
    cos, sin = cos.T, sin.T
    backward_z = np.block([[cos, sin], [-sin, cos]])
    k = np.arange(GX)
    forward_x = []
    for p in range(3):
        angle = 2 * np.pi * ((k[:, None] * (3 * np.arange(128)[None, :] + p)) % GX) / GX
        forward_x += [np.cos(angle), np.sin(angle)]
    backward_x = np.concatenate(
        [np.concatenate([forward_x[2 * p].T, forward_x[2 * p + 1].T], 1) for p in range(3)], 0
    )
    forward_x = np.concatenate(forward_x, 1)
    flip_x = np.eye(GX)[:, -np.arange(GX) % GX]
    flip_z = np.eye(GZ)[:, -np.arange(GZ) % GZ]
    out = [flip_x.astype(bf16), flip_z.astype(bf16)]
    for table in (forward_y, forward_x, forward_z, backward_z, backward_x, backward_y):
        out += list(halves(table))
    return out


def split(x):
    high = x.astype(bf16)
    return high, (x - high.astype(f32)).astype(bf16)


def nn(a, b):
    return lax.dot_general(a, b, (((1,), (0,)), ((), ())), preferred_element_type=f32)


def nt(a, b):
    return lax.dot_general(a, b, (((1,), (1,)), ((), ())), preferred_element_type=f32)


def left(table_high, table_low, x):
    high, low = split(x)
    return nn(
        jnp.concatenate([table_high, table_high, table_low], 1),
        jnp.concatenate([high, low, high], 0),
    )


def right(x, table_high, table_low):
    high, low = split(x)
    return nn(
        jnp.concatenate([high, low, high], 1),
        jnp.concatenate([table_high, table_high, table_low], 0),
    )


FINE_Y, FINE_Z = 72, 7
PATCH = 512


def step_masks(base, n):
    it = lax.broadcasted_iota(jnp.int32, (FINE_Y, n), 0)
    return [it == base + k for k in range(4)]


def one_hot(row, column):
    it = lax.broadcasted_iota(jnp.int32, (256, row.shape[1]), 0)
    return jnp.where(it == (row >> 6) * 64 + (column >> 2), 1.0, 0.0).astype(bf16)


def pick(masks, w):
    r = jnp.where(masks[3], w[3], jnp.zeros((), w[0].dtype))
    for k in (2, 1, 0):
        r = jnp.where(masks[k], w[k], r)
    return r


def plane_weights(local, w, step):
    step = step - local
    r = jnp.zeros_like(w[0])
    for k in range(4):
        r = jnp.where(step == k, w[k], r)
    return r


class Atoms:
    def __init__(self, shift, first, dipoles, values, slopes, plane, row, column):
        self.shift, self.first = shift, first
        self.refs = (dipoles, values, slopes, plane, row, column)

    def read(self, start):
        cols = pl.ds(pl.multiple_of(start, CHUNK), CHUNK)
        dipoles, values, slopes, plane, row, column = self.refs
        m = [dipoles[a : a + 1, cols] for a in range(3)]
        v = [[values[a, k : k + 1, cols] for k in range(4)] for a in range(3)]
        s = [[slopes[a, k : k + 1, cols] for k in range(4)] for a in range(3)]
        return row[:, cols], column[:, cols], plane[:, cols] - self.first, m, v, s


def fine_tables(row, column, v, s):
    at_y = step_masks(row & 63, row.shape[1])
    column = column & 3
    at_z = lambda w: [plane_weights(column, w, f) for f in range(FINE_Z)]
    return pick(at_y, v[1]), pick(at_y, s[1]), at_z(v[2]), at_z(s[2])


def spread_chunk(cell, start, planes, patches):
    row, column, local, m, v, s = cell.read(start)
    v1, s1, v2, s2 = fine_tables(row, column, v, s)
    hot = one_hot(row, column)
    hot = jnp.concatenate([hot, hot], 1)
    for p in planes:
        x0 = plane_weights(local, v[0], p + cell.shift)
        xs = plane_weights(local, s[0], p + cell.shift)
        a = v1 * (m[0] * xs) + s1 * (m[1] * x0)
        b = v1 * (m[2] * x0)
        w = [a * v2[f] + b * s2[f] for f in range(FINE_Z)] + [jnp.zeros((8, CHUNK), f32)]
        high, low = split(jnp.concatenate(w, 0))
        patches[p] += nt(jnp.concatenate([high, low], 1), hot)


def roll_columns(x, step):
    lane = lax.broadcasted_iota(jnp.int32, (x.shape[0], 128), 1) & 63
    out = []
    for h in range(2):
        part = x[:, h * 128 : h * 128 + 128]
        wrapped = lane == (0 if step == 1 else 63)
        out.append(
            jnp.where(
                wrapped, pltpu.roll(part, 65 if step == 1 else 63, 1), pltpu.roll(part, step % 128, 1)
            )
        )
    return jnp.concatenate(out, 1)


def swap_parts(blocks):
    first = lax.broadcasted_iota(jnp.int32, (blocks[0].shape[0], 128), 1) < 64
    half = [[x[:, h * 128 : h * 128 + 128] for h in range(2)] for x in blocks]
    turned = [[pltpu.roll(x, 64, 1) for x in pair] for pair in half]
    out = []
    for part in range(4):
        h, odd = part // 2, part % 2
        row = []
        for g in range(2):
            even_block, odd_block = 2 * g, 2 * g + 1
            if odd:
                row.append(jnp.where(first, turned[even_block][h], half[odd_block][h]))
            else:
                row.append(jnp.where(first, half[even_block][h], turned[odd_block][h]))
        out.append(jnp.concatenate(row, 1))
    return out


def patches_to_grid(patches, p, grid):
    t = [patches[p, f * FINE_Y : f * FINE_Y + FINE_Y, :] for f in range(FINE_Z)]
    t = [t[f] + roll_columns(t[f + 4], 1) if f < 3 else t[f] for f in range(4)]
    grid[...] = jnp.zeros_like(grid)
    for yb, x in enumerate(swap_parts(t)):
        grid[64 * yb : 64 * yb + FINE_Y, :] += x
    grid[0:8, :] += grid[256:264, :]
    return grid[0:256, :]


def grid_to_patches(pot, grid, stacked, p):
    grid[...] = pot
    t = swap_parts([grid[64 * yb : 64 * yb + FINE_Y, :] for yb in range(4)])
    t = t + [roll_columns(t[f], -1) for f in range(3)] + [jnp.zeros((8, 256), f32)]
    high, low = split(jnp.concatenate(t, 0))
    stacked[p] = jnp.concatenate([high, low], 1)


def sample_chunk(cell, start, planes, stacked, out):
    row, column, local, m, v, s = cell.read(start)
    v1, s1, v2, s2 = fine_tables(row, column, v, s)
    hot = one_hot(row, column)
    hot = jnp.concatenate([hot, hot], 0)
    total = jnp.zeros((3, CHUNK), f32)
    for p in planes:
        x0 = plane_weights(local, v[0], p + cell.shift)
        xs = plane_weights(local, s[0], p + cell.shift)
        t = nn(stacked[p], hot)
        tv = ts = 0.0
        for f in range(FINE_Z):
            part = t[f * FINE_Y : f * FINE_Y + FINE_Y]
            tv, ts = tv + part * v2[f], ts + part * s2[f]
        r = [
            xs * jnp.sum(v1 * tv, 0, keepdims=True),
            x0 * jnp.sum(s1 * tv, 0, keepdims=True),
            x0 * jnp.sum(v1 * ts, 0, keepdims=True),
        ]
        total = total + jnp.concatenate(r, 0)
    out[:, pl.ds(pl.multiple_of(start, CHUNK), CHUNK)] -= total


def extend(parts, ext):
    for part, (positions, dipoles) in enumerate(parts):
        for c in range(CLU_DEV):
            cols = slice(c * CL, c * CL + CL)
            x = positions[:, cols]
            if part != 1:
                shift = 2.0 * (part - 1)
                x = x + jnp.where(lax.broadcasted_iota(jnp.int32, (3, CL), 0) == 0, shift, 0.0)
            ext[part * CLU_DEV + c, 0:3, :] = x
            ext[part * CLU_DEV + c, 3:6, :] = dipoles[:, cols]


def direct_slots(lo, hi, home, other, count, ext, acc):
    eye = (
        lax.broadcasted_iota(jnp.int32, (CL, CL), 0) == lax.broadcasted_iota(jnp.int32, (CL, CL), 1)
    ).astype(f32)
    which = lax.broadcasted_iota(jnp.int32, (CLU_DEV, 8, CL), 0)

    def slot(t, carry):
        h, o = home[t], other[t]
        hx = ext[h + CLU_DEV]
        ox = ext[o].T
        delta = [hx[a : a + 1, :] - ox[:, a : a + 1] for a in range(3)]
        m = [ox[:, 3 + a : 4 + a] for a in range(3)]
        q = delta[0] * delta[0] + delta[1] * delta[1] + delta[2] * delta[2]
        inverse = lax.rsqrt(q + 0.25)
        square = inverse * inverse
        self_slot = jnp.where(o == h + CLU_DEV, 1.0, 0.0)
        first = jnp.exp(-0.5 * q) * (inverse * square) * (1.0 - self_slot * eye)
        second = 3.0 * first * square
        along = second * (delta[0] * m[0] + delta[1] * m[1] + delta[2] * m[2])
        e = [jnp.sum(along * delta[a] - first * m[a], 0, keepdims=True) for a in range(3)]
        live = jnp.where(t < count[0], 0.125, 0.0)
        e = jnp.concatenate(e + [jnp.zeros((5, CL), f32)], 0) * live
        acc[...] += jnp.where(which == h, e[None], 0.0)
        return carry

    lax.fori_loop(lo, hi, slot, 0, unroll=4)


def device_id(t):
    return (t >> 6, t & 63)


def remote(src, dst, send_sem, recv_sem, t):
    return pltpu.make_async_remote_copy(
        src_ref=src,
        dst_ref=dst,
        send_sem=send_sem,
        recv_sem=recv_sem,
        device_id=device_id(t),
        device_id_type=pl.DeviceIdType.MESH,
    )


def exchange_start(me, p, src, dst, send_sem, recv_sem):
    def send(i, c):
        t = (me + i) & (DEV - 1)
        remote(src.at[p, t], dst.at[p, me], send_sem.at[p], recv_sem.at[p], t).start()
        return c

    lax.fori_loop(1, DEV, send, 0, unroll=8)
    dst[p, pl.ds(me, 1)] = src[p, pl.ds(me, 1)]


def exchange_wait(p, src, sem):
    part = src.at[p, pl.ds(0, DEV - 1)]
    pltpu.make_async_copy(part, part, sem.at[p]).wait()


def to_rows(ref, p, value):
    view = ref.at[p].reshape(512, 128)
    for c in range(2):
        for h in range(2):
            view[pl.ds(2 * c + h, 128, stride=4), :] = value[
                c * 128 : c * 128 + 128, h * 128 : h * 128 + 128
            ]


def from_rows(ref, p):
    view = ref.at[p].reshape(512, 128)
    part = [view[pl.ds(k, 128, stride=4), :] for k in range(4)]
    return jnp.concatenate(part[0:2], 1), jnp.concatenate(part[2:4], 1)


def flipped(x, flip_x, flip_z):
    high, low = split(x)
    y = nn(flip_x, jnp.concatenate([high, low], 1))
    high, low = split(y[:, 0:GZ] + y[:, GZ:])
    y = nn(jnp.concatenate([high, low], 0), flip_z)
    return y[0:GX] + y[GX:]


N_TABLES = 14
N_ATOM = 7


def kernel(*refs):
    refs = list(refs)
    take = lambda n: [refs.pop(0) for _ in range(n)]
    home, other, count = take(3)
    own_refs = take(N_ATOM)
    influence, *table_hbm = take(1 + N_TABLES)
    (out,) = take(1)
    before_refs = take(N_ATOM)
    after_refs = take(2)
    table = take(N_TABLES)
    rows_in, sent, got, keep, turn = take(5)
    send1, recv1, send2, recv2, spec, other_spec, grid, ext, acc, out_before, returned = take(11)
    patches, stacked = take(2)
    ss1, rs1, ss2, rs2, atom_ss, atom_rs, table_sem, rows_sem, infl_sem, back_sem = take(10)

    me = lax.axis_index("grp") * 64 + lax.axis_index("sp")
    above, below = lax.rem(me + 1, DEV), lax.rem(me + DEV - 1, DEV)
    loads = [
        pltpu.make_async_copy(a, b, table_sem.at[i])
        for i, (a, b) in enumerate(zip(table_hbm, table))
    ]
    rows_load = pltpu.make_async_copy(influence, rows_in, rows_sem)
    rows_load.start()
    for load in loads:
        load.start()
    barrier = pltpu.get_barrier_semaphore()

    def greet(i, c):
        pl.semaphore_signal(
            barrier,
            inc=1,
            device_id=device_id((me + i) & (DEV - 1)),
            device_id_type=pl.DeviceIdType.MESH,
        )
        return c

    lax.fori_loop(1, DEV, greet, 0, unroll=4)
    own = Atoms(0, 3 * me, *own_refs[1:])
    before = Atoms(3, 3 * below, *before_refs[1:])
    chunks = ATOM_DEV // CHUNK

    def loop(lo, hi, f):
        def step(i, c):
            f(i * CHUNK)
            return c

        lax.fori_loop(lo, hi, step, 0)

    patches[...] = jnp.zeros_like(patches)
    out[...] = jnp.zeros_like(out)
    out_before[...] = jnp.zeros_like(out_before)
    acc[...] = jnp.zeros_like(acc)
    ext[...] = jnp.zeros_like(ext)
    loop(0, 2, lambda start: spread_chunk(own, start, range(3), patches))

    pl.semaphore_wait(barrier, DEV - 1)
    copies = [
        remote(a, b, atom_ss.at[i], atom_rs.at[i], above)
        for i, (a, b) in enumerate(zip(own_refs, before_refs))
    ]
    copies += [
        remote(a, b, atom_ss.at[N_ATOM + i], atom_rs.at[N_ATOM + i], below)
        for i, (a, b) in enumerate(zip(own_refs[:2], after_refs))
    ]
    for copy in copies:
        copy.start()
    rows_load.wait()
    lower = me < 64
    sent[...] = jnp.where(lower, rows_in[:, 1, :], rows_in[:, 0, :])
    target = jnp.where(lower, 127 - me, lax.rem(DEV - me, 64))
    infl_copy = remote(sent, got, infl_sem.at[0], infl_sem.at[1], target)
    infl_copy.start()

    loop(2, chunks, lambda start: spread_chunk(own, start, range(3), patches))
    for copy in copies:
        copy.wait()
    for load in loads:
        load.wait()
    flip_x, flip_z, fyh, fyl, fxh, fxl, fzh, fzl, bzh, bzl, bxh, bxl, byh, byl = table
    loop(0, chunks, lambda start: spread_chunk(before, start, range(3), patches))
    for p in range(3):
        to_rows(send1, p, left(fyh[...], fyl[...], patches_to_grid(patches, p, grid)))
        exchange_start(me, p, send1, recv1, ss1, rs1)

    extend(
        ((before_refs[0], before_refs[1]), (own_refs[0], own_refs[1]), (after_refs[0], after_refs[1])), ext
    )
    direct_slots(0, SLOTS // 2, home, other, count, ext, acc)
    infl_copy.wait()
    kept = jnp.where(lower, rows_in[:, 0, :], rows_in[:, 1, :])
    u, v = jnp.where(lower, kept, got[...]), jnp.where(lower, got[...], kept)
    same, turned = 0.5 * u, 0.5 * v
    both = 0.25 * (u + v)
    first = me == 0
    keep[...] = jnp.where(first, both, same) + flipped(
        jnp.where(first, both, turned), flip_x[...], flip_z[...]
    )

    @pl.when(first)
    def _():
        q = 0.25 * (rows_in[:, 0, :] - got[...])
        turn[...] = q + flipped(q, flip_x[...], flip_z[...])

    for p in range(3):
        exchange_wait(p, recv1, rs1)
        cols = slice(p * 256, p * 256 + 256)

        def stage(sign):
            real, imag = from_rows(recv1, p)
            imag = imag * sign
            x = jnp.concatenate(
                [jnp.concatenate([real, imag], 1), jnp.concatenate([imag, -real], 1)], 0
            )
            return left(fxh[:, cols], fxl[:, cols], x)

        if p == 0:
            spec[...] = stage(1.0)
        else:
            spec[...] += stage(1.0)

        @pl.when(first)
        def _():
            if p == 0:
                other_spec[...] = stage(-1.0)
            else:
                other_spec[...] += stage(-1.0)

    twice = lambda x: jnp.concatenate([x, x], 1)
    spec[...] = right(spec[...], fzh[...], fzl[...]) * twice(keep[...])

    @pl.when(first)
    def _():
        spec[...] += right(other_spec[...], fzh[...], fzl[...]) * twice(turn[...])

    back = right(spec[...], bzh[...], bzl[...])
    real, imag = back[:, 0:256], back[:, 256:512]
    x = jnp.concatenate([jnp.concatenate([real, imag], 1), jnp.concatenate([-imag, real], 1)], 0)
    high, low = split(x)
    x = jnp.concatenate([high, low, high], 0)
    for p in range(3):
        rows = slice(p * 128, p * 128 + 128)
        y = nn(jnp.concatenate([bxh[rows, :], bxh[rows, :], bxl[rows, :]], 1), x)
        to_rows(send2, p, jnp.concatenate([y[:, 0:256], y[:, 256:512]], 0))
        exchange_start(me, p, send2, recv2, ss2, rs2)

    direct_slots(SLOTS // 2, SLOTS, home, other, count, ext, acc)
    back_copy = remote(out_before, returned, back_sem.at[0], back_sem.at[1], below)
    for p in range(3):
        exchange_wait(p, recv2, rs2)
        real, imag = from_rows(recv2, p)
        pot = left(byh[...], byl[...], jnp.concatenate([real, imag], 0))
        grid_to_patches(pot, grid, stacked, p)
    loop(0, chunks, lambda start: sample_chunk(before, start, range(3), stacked, out_before))
    back_copy.start()
    loop(0, chunks, lambda start: sample_chunk(own, start, range(3), stacked, out))
    back_copy.wait()
    for c in range(CLU_DEV):
        cols = slice(c * CL, c * CL + CL)
        out[:, cols] += returned[:, cols] + acc[c, 0:3, :]
    for p in range(3):
        exchange_wait(p, send1, ss1)
        exchange_wait(p, send2, ss2)


def on_device(
    positions,
    dipoles,
    spline_values,
    spline_slopes,
    plane_base,
    row_base,
    column_base,
    pair_home,
    pair_other,
    pair_count,
    influence,
):
    constants = [jnp.asarray(t) for t in tables()]
    own = [
        positions,
        dipoles,
        spline_values,
        spline_slopes,
        plane_base.reshape(1, ATOM_DEV),
        row_base.reshape(1, ATOM_DEV),
        column_base.reshape(1, ATOM_DEV),
    ]
    vm = lambda x: pltpu.VMEM(x.shape, x.dtype)
    blocks = pltpu.VMEM((3, DEV, 4, 128), f32)
    return pl.pallas_call(
        kernel,
        out_shape=jax.ShapeDtypeStruct((3, ATOM_DEV), f32),
        in_specs=[SM] * 3 + [VM] * N_ATOM + [pl.BlockSpec(memory_space=pltpu.HBM)] * (1 + N_TABLES),
        out_specs=VM,
        scratch_shapes=[vm(x) for x in own]
        + [vm(x) for x in own[:2]]
        + [vm(x) for x in constants]
        + [pltpu.VMEM((GX, 2, GZ), f32)]
        + [pltpu.VMEM((GX, GZ), f32)] * 4
        + [blocks] * 4
        + [pltpu.VMEM((GX, 512), f32)] * 2
        + [
            pltpu.VMEM((272, 256), f32),
            pltpu.VMEM((48, 8, CL), f32),
            pltpu.VMEM((CLU_DEV, 8, CL), f32),
            pltpu.VMEM((3, ATOM_DEV), f32),
            pltpu.VMEM((3, ATOM_DEV), f32),
        ]
        + [pltpu.VMEM((3, PATCH, 256), f32), pltpu.VMEM((3, PATCH, 512), bf16)]
        + [pltpu.SemaphoreType.DMA((3,))] * 4
        + [pltpu.SemaphoreType.DMA((N_ATOM + 2,))] * 2
        + [pltpu.SemaphoreType.DMA((N_TABLES,)), pltpu.SemaphoreType.DMA]
        + [pltpu.SemaphoreType.DMA((2,))] * 2,
        compiler_params=pltpu.CompilerParams(
            vmem_limit_bytes=62 << 20, collective_id=0, has_side_effects=True
        ),
        name="polarization",
    )(pair_home, pair_other, pair_count, *own, influence, *constants)


def solution(mesh):
    placed = (
        P(None, AXES),
        P(None, AXES),
        P(None, None, AXES),
        P(None, None, AXES),
        P(AXES),
        P(AXES),
        P(AXES),
        P(AXES),
        P(AXES),
        P(AXES),
        P(None, AXES, None),
    )
    return jax.shard_map(
        on_device, mesh=mesh, in_specs=placed, out_specs=P(None, AXES), check_vma=False
    )
```

```python
import functools

import jax
import jax.numpy as jnp
import numpy as np
from jax import lax
from jax.experimental import pallas as pl
from jax.experimental.pallas import tpu as pltpu
from jax.sharding import PartitionSpec as P

CL = 128
CLU_DEV = 16
GX = 384
GY = 256
GZ = 256
DEV = 128
ATOM_DEV = 2048
SLOTS = 32
CHUNK = 1024
SAMPLE = 1024
AXES = ("grp", "sp")

f32, bf16 = jnp.float32, jnp.bfloat16
VM = pl.BlockSpec(memory_space=pltpu.VMEM)
SM = pl.BlockSpec(memory_space=pltpu.SMEM)


def halves(table):
    high = table.astype(bf16)
    low = (table - high.astype(np.float64)).astype(bf16)
    return high, low


@functools.cache
def tables():
    t = np.arange(128)[:, None]
    d = np.where(t < 64, 2 * t, 255 - 2 * t)
    y = np.arange(GY)[None, :]
    angle = 2 * np.pi * ((d * y) % GY) / GY
    real, imag = np.cos(angle), -np.sin(angle)
    imag[0] = 1 - 2 * (np.arange(GY) % 2)
    forward_y = np.concatenate([real, imag], 0)
    scale = np.full((1, 256), 2.0)
    scale[0, 0] = scale[0, 128] = 1.0
    backward_y = forward_y.T * scale / (GX * GY * GZ)
    backward_y = np.concatenate([backward_y, backward_y[:16]], 0)
    z = np.arange(GZ)
    angle = 2 * np.pi * ((z[:, None] * z[None, :]) % GZ) / GZ
    cos, sin = np.cos(angle), np.sin(angle)
    order = 4 * (z % 64) + z // 64
    cos, sin = cos[order], sin[order]
    forward_z = np.block([[cos, -sin], [sin, cos]])
    cos, sin = cos.T, sin.T
    backward_z = np.block([[cos, sin], [-sin, cos]])
    k = np.arange(GX)
    forward_x = []
    for p in range(3):
        angle = 2 * np.pi * ((k[:, None] * (3 * np.arange(128)[None, :] + p)) % GX) / GX
        forward_x += [np.cos(angle), np.sin(angle)]
    backward_x = np.concatenate(
        [np.concatenate([forward_x[2 * p].T, forward_x[2 * p + 1].T], 1) for p in range(3)], 0
    )
    forward_x = np.concatenate(forward_x, 1)
    flip_x = np.eye(GX)[:, -np.arange(GX) % GX]
    flip_z = np.eye(GZ)[:, -np.arange(GZ) % GZ]
    out = [flip_x.astype(bf16), flip_z.astype(bf16)]
    for table in (forward_y, forward_x, forward_z, backward_z, backward_x, backward_y):
        out += list(halves(table))
    return out


def split(x):
    high = x.astype(bf16)
    return high, (x - high.astype(f32)).astype(bf16)


def nn(a, b):
    return lax.dot_general(a, b, (((1,), (0,)), ((), ())), preferred_element_type=f32)


def nt(a, b):
    return lax.dot_general(a, b, (((1,), (1,)), ((), ())), preferred_element_type=f32)


def left(table_high, table_low, x):
    high, low = split(x)
    return nn(
        jnp.concatenate([table_high, table_high, table_low], 1),
        jnp.concatenate([high, low, high], 0),
    )


def right(x, table_high, table_low):
    high, low = split(x)
    return nn(
        jnp.concatenate([high, low, high], 1),
        jnp.concatenate([table_high, table_high, table_low], 0),
    )


FINE_Y, FINE_Z = 72, 7
PATCH = 512


def step_masks(base, n):
    it = lax.broadcasted_iota(jnp.int32, (FINE_Y, n), 0)
    return [it == base + k for k in range(4)]


def one_hot(row, column):
    it = lax.broadcasted_iota(jnp.int32, (256, row.shape[1]), 0)
    return jnp.where(it == (row >> 6) * 64 + (column >> 2), 1.0, 0.0).astype(bf16)


def pick(masks, w):
    r = jnp.where(masks[3], w[3], jnp.zeros((), w[0].dtype))
    for k in (2, 1, 0):
        r = jnp.where(masks[k], w[k], r)
    return r


def plane_weights(local, w, step):
    step = step - local
    r = jnp.zeros_like(w[0])
    for k in range(4):
        r = jnp.where(step == k, w[k], r)
    return r


class Atoms:
    def __init__(self, shift, first, dipoles, values, slopes, plane, row, column):
        self.shift, self.first = shift, first
        self.refs = (dipoles, values, slopes, plane, row, column)

    def read(self, start, n):
        cols = pl.ds(pl.multiple_of(start, n), n)
        dipoles, values, slopes, plane, row, column = self.refs
        m = [dipoles[a : a + 1, cols] for a in range(3)]
        v = [[values[a, k : k + 1, cols] for k in range(4)] for a in range(3)]
        s = [[slopes[a, k : k + 1, cols] for k in range(4)] for a in range(3)]
        return row[:, cols], column[:, cols], plane[:, cols] - self.first, m, v, s


def fine_tables(row, column, v, s):
    at_y = step_masks(row & 63, row.shape[1])
    column = column & 3
    at_z = lambda w: [plane_weights(column, w, f) for f in range(FINE_Z)]
    return pick(at_y, v[1]), pick(at_y, s[1]), at_z(v[2]), at_z(s[2])


def spread_chunk(cell, start, planes, patches):
    row, column, local, m, v, s = cell.read(start, CHUNK)
    v1, s1, v2, s2 = fine_tables(row, column, v, s)
    hot = one_hot(row, column)
    hot = jnp.concatenate([hot, hot], 1)
    for p in planes:
        x0 = plane_weights(local, v[0], p + cell.shift)
        xs = plane_weights(local, s[0], p + cell.shift)
        a = v1 * (m[0] * xs) + s1 * (m[1] * x0)
        b = v1 * (m[2] * x0)
        w = [a * v2[f] + b * s2[f] for f in range(FINE_Z)] + [jnp.zeros((8, CHUNK), f32)]
        high, low = split(jnp.concatenate(w, 0))
        patches[p] += nt(jnp.concatenate([high, low], 1), hot)


def roll_columns(x, step):
    lane = lax.broadcasted_iota(jnp.int32, (x.shape[0], 128), 1) & 63
    out = []
    for h in range(2):
        part = x[:, h * 128 : h * 128 + 128]
        wrapped = lane == (0 if step == 1 else 63)
        out.append(
            jnp.where(
                wrapped, pltpu.roll(part, 65 if step == 1 else 63, 1), pltpu.roll(part, step % 128, 1)
            )
        )
    return jnp.concatenate(out, 1)


def swap_parts(blocks):
    first = lax.broadcasted_iota(jnp.int32, (blocks[0].shape[0], 128), 1) < 64
    half = [[x[:, h * 128 : h * 128 + 128] for h in range(2)] for x in blocks]
    turned = [[pltpu.roll(x, 64, 1) for x in pair] for pair in half]
    out = []
    for part in range(4):
        h, odd = part // 2, part % 2
        row = []
        for g in range(2):
            even_block, odd_block = 2 * g, 2 * g + 1
            if odd:
                row.append(jnp.where(first, turned[even_block][h], half[odd_block][h]))
            else:
                row.append(jnp.where(first, half[even_block][h], turned[odd_block][h]))
        out.append(jnp.concatenate(row, 1))
    return out


def patches_to_grid(patches, p, grid):
    t = [patches[p, f * FINE_Y : f * FINE_Y + FINE_Y, :] for f in range(FINE_Z)]
    t = [t[f] + roll_columns(t[f + 4], 1) if f < 3 else t[f] for f in range(4)]
    grid[...] = jnp.zeros_like(grid)
    for yb, x in enumerate(swap_parts(t)):
        grid[64 * yb : 64 * yb + FINE_Y, :] += x
    grid[0:8, :] += grid[256:264, :]
    return grid[0:256, :]


def grid_to_patches(pot, grid, stacked, p):
    grid[...] = pot
    t = swap_parts([grid[64 * yb : 64 * yb + FINE_Y, :] for yb in range(4)])
    t = t + [roll_columns(t[f], -1) for f in range(3)] + [jnp.zeros((8, 256), f32)]
    high, low = split(jnp.concatenate(t, 0))
    stacked[p] = jnp.concatenate([high, low], 1)


def sample_chunk(cell, start, planes, stacked, out):
    row, column, local, m, v, s = cell.read(start, SAMPLE)
    v1, s1, v2, s2 = fine_tables(row, column, v, s)
    hot = one_hot(row, column)
    hot = jnp.concatenate([hot, hot], 0)
    total = jnp.zeros((3, SAMPLE), f32)
    for p in planes:
        x0 = plane_weights(local, v[0], p + cell.shift)
        xs = plane_weights(local, s[0], p + cell.shift)
        t = nn(stacked[p], hot)
        tv = ts = 0.0
        for f in range(FINE_Z):
            part = t[f * FINE_Y : f * FINE_Y + FINE_Y]
            tv, ts = tv + part * v2[f], ts + part * s2[f]
        r = [
            xs * jnp.sum(v1 * tv, 0, keepdims=True),
            x0 * jnp.sum(s1 * tv, 0, keepdims=True),
            x0 * jnp.sum(v1 * ts, 0, keepdims=True),
        ]
        total = total + jnp.concatenate(r, 0)
    out[:, pl.ds(pl.multiple_of(start, SAMPLE), SAMPLE)] -= total


def extend(parts, ext):
    for part, (positions, dipoles) in enumerate(parts):
        for c in range(CLU_DEV):
            cols = slice(c * CL, c * CL + CL)
            x = positions[:, cols]
            if part != 1:
                shift = 2.0 * (part - 1)
                x = x + jnp.where(lax.broadcasted_iota(jnp.int32, (3, CL), 0) == 0, shift, 0.0)
            ext[part * CLU_DEV + c, 0:3, :] = x
            ext[part * CLU_DEV + c, 3:6, :] = dipoles[:, cols]


def direct_slots(lo, hi, home, other, count, ext, acc):
    eye = (
        lax.broadcasted_iota(jnp.int32, (CL, CL), 0) == lax.broadcasted_iota(jnp.int32, (CL, CL), 1)
    ).astype(f32)
    which = lax.broadcasted_iota(jnp.int32, (CLU_DEV, 8, CL), 0)

    def slot(t, carry):
        h, o = home[t], other[t]
        hx = ext[h + CLU_DEV]
        ox = ext[o].T
        delta = [hx[a : a + 1, :] - ox[:, a : a + 1] for a in range(3)]
        m = [ox[:, 3 + a : 4 + a] for a in range(3)]
        q = delta[0] * delta[0] + delta[1] * delta[1] + delta[2] * delta[2]
        inverse = lax.rsqrt(q + 0.25)
        square = inverse * inverse
        self_slot = jnp.where(o == h + CLU_DEV, 1.0, 0.0)
        first = jnp.exp(-0.5 * q) * (inverse * square) * (1.0 - self_slot * eye)
        second = 3.0 * first * square
        along = second * (delta[0] * m[0] + delta[1] * m[1] + delta[2] * m[2])
        e = [jnp.sum(along * delta[a] - first * m[a], 0, keepdims=True) for a in range(3)]
        live = jnp.where(t < count[0], 0.125, 0.0)
        e = jnp.concatenate(e + [jnp.zeros((5, CL), f32)], 0) * live
        acc[...] += jnp.where(which == h, e[None], 0.0)
        return carry

    lax.fori_loop(lo, hi, slot, 0, unroll=4)


def device_id(t):
    return (t >> 6, t & 63)


def remote(src, dst, send_sem, recv_sem, t):
    return pltpu.make_async_remote_copy(
        src_ref=src,
        dst_ref=dst,
        send_sem=send_sem,
        recv_sem=recv_sem,
        device_id=device_id(t),
        device_id_type=pl.DeviceIdType.MESH,
    )


def exchange_start(me, p, src, dst, send_sem, recv_sem):
    def send(i, c):
        t = (me + i) & (DEV - 1)
        remote(src.at[p, t], dst.at[p, me], send_sem.at[p], recv_sem.at[p], t).start()
        return c

    lax.fori_loop(1, DEV, send, 0, unroll=8)
    dst[p, pl.ds(me, 1)] = src[p, pl.ds(me, 1)]


def exchange_wait(p, src, sem):
    part = src.at[p, pl.ds(0, DEV - 1)]
    pltpu.make_async_copy(part, part, sem.at[p]).wait()


def to_rows(ref, p, value):
    view = ref.at[p].reshape(512, 128)
    for c in range(2):
        for h in range(2):
            view[pl.ds(2 * c + h, 128, stride=4), :] = value[
                c * 128 : c * 128 + 128, h * 128 : h * 128 + 128
            ]


def from_rows(ref, p):
    view = ref.at[p].reshape(512, 128)
    part = [view[pl.ds(k, 128, stride=4), :] for k in range(4)]
    return jnp.concatenate(part[0:2], 1), jnp.concatenate(part[2:4], 1)


def flipped(x, flip_x, flip_z):
    high, low = split(x)
    y = nn(flip_x, jnp.concatenate([high, low], 1))
    high, low = split(y[:, 0:GZ] + y[:, GZ:])
    y = nn(jnp.concatenate([high, low], 0), flip_z)
    return y[0:GX] + y[GX:]


N_TABLES = 14
N_ATOM = 7


def kernel(*refs):
    refs = list(refs)
    take = lambda n: [refs.pop(0) for _ in range(n)]
    home, other, count = take(3)
    own_refs = take(N_ATOM)
    influence, *table_hbm = take(1 + N_TABLES)
    (out,) = take(1)
    before_refs = take(N_ATOM)
    after_refs = take(2)
    table = take(N_TABLES)
    rows_in, sent, got, keep, turn = take(5)
    send1, recv1, send2, recv2, spec, other_spec, grid, ext, acc, out_before, returned = take(11)
    patches, stacked = take(2)
    ss1, rs1, ss2, rs2, atom_ss, atom_rs, table_sem, rows_sem, infl_sem, back_sem = take(10)

    me = lax.axis_index("grp") * 64 + lax.axis_index("sp")
    above, below = lax.rem(me + 1, DEV), lax.rem(me + DEV - 1, DEV)
    loads = [
        pltpu.make_async_copy(a, b, table_sem.at[i])
        for i, (a, b) in enumerate(zip(table_hbm, table))
    ]
    rows_load = pltpu.make_async_copy(influence, rows_in, rows_sem)
    rows_load.start()
    for load in loads:
        load.start()
    barrier = pltpu.get_barrier_semaphore()

    def greet(i, c):
        pl.semaphore_signal(
            barrier,
            inc=1,
            device_id=device_id((me + i) & (DEV - 1)),
            device_id_type=pl.DeviceIdType.MESH,
        )
        return c

    lax.fori_loop(1, DEV, greet, 0, unroll=4)
    own = Atoms(0, 3 * me, *own_refs[1:])
    before = Atoms(3, 3 * below, *before_refs[1:])
    chunks = ATOM_DEV // CHUNK

    def loop(lo, hi, f, n=CHUNK):
        def step(i, c):
            f(i * n)
            return c

        lax.fori_loop(lo, hi, step, 0)

    patches[...] = jnp.zeros_like(patches)
    out[...] = jnp.zeros_like(out)
    out_before[...] = jnp.zeros_like(out_before)
    acc[...] = jnp.zeros_like(acc)
    ext[...] = jnp.zeros_like(ext)
    loop(0, chunks // 2, lambda start: spread_chunk(own, start, range(3), patches))

    pl.semaphore_wait(barrier, DEV - 1)
    copies = [
        remote(a, b, atom_ss.at[i], atom_rs.at[i], above)
        for i, (a, b) in enumerate(zip(own_refs, before_refs))
    ]
    copies += [
        remote(a, b, atom_ss.at[N_ATOM + i], atom_rs.at[N_ATOM + i], below)
        for i, (a, b) in enumerate(zip(own_refs[:2], after_refs))
    ]
    for copy in copies:
        copy.start()
    rows_load.wait()
    lower = me < 64
    sent[...] = jnp.where(lower, rows_in[:, 1, :], rows_in[:, 0, :])
    target = jnp.where(lower, 127 - me, lax.rem(DEV - me, 64))
    infl_copy = remote(sent, got, infl_sem.at[0], infl_sem.at[1], target)
    infl_copy.start()

    loop(chunks // 2, chunks, lambda start: spread_chunk(own, start, range(3), patches))
    for copy in copies:
        copy.wait()
    for load in loads:
        load.wait()
    flip_x, flip_z, fyh, fyl, fxh, fxl, fzh, fzl, bzh, bzl, bxh, bxl, byh, byl = table
    loop(0, chunks, lambda start: spread_chunk(before, start, range(3), patches))
    for p in range(3):
        to_rows(send1, p, left(fyh[...], fyl[...], patches_to_grid(patches, p, grid)))
        exchange_start(me, p, send1, recv1, ss1, rs1)

    extend(
        ((before_refs[0], before_refs[1]), (own_refs[0], own_refs[1]), (after_refs[0], after_refs[1])), ext
    )
    direct_slots(0, SLOTS // 2, home, other, count, ext, acc)
    infl_copy.wait()
    kept = jnp.where(lower, rows_in[:, 0, :], rows_in[:, 1, :])
    u, v = jnp.where(lower, kept, got[...]), jnp.where(lower, got[...], kept)
    same, turned = 0.5 * u, 0.5 * v
    both = 0.25 * (u + v)
    first = me == 0
    keep[...] = jnp.where(first, both, same) + flipped(
        jnp.where(first, both, turned), flip_x[...], flip_z[...]
    )

    @pl.when(first)
    def _():
        q = 0.25 * (rows_in[:, 0, :] - got[...])
        turn[...] = q + flipped(q, flip_x[...], flip_z[...])

    for p in range(3):
        exchange_wait(p, recv1, rs1)
        cols = slice(p * 256, p * 256 + 256)

        def stage(sign):
            real, imag = from_rows(recv1, p)
            imag = imag * sign
            x = jnp.concatenate(
                [jnp.concatenate([real, imag], 1), jnp.concatenate([imag, -real], 1)], 0
            )
            return left(fxh[:, cols], fxl[:, cols], x)

        if p == 0:
            spec[...] = stage(1.0)
        else:
            spec[...] += stage(1.0)

        @pl.when(first)
        def _():
            if p == 0:
                other_spec[...] = stage(-1.0)
            else:
                other_spec[...] += stage(-1.0)

    twice = lambda x: jnp.concatenate([x, x], 1)
    spec[...] = right(spec[...], fzh[...], fzl[...]) * twice(keep[...])

    @pl.when(first)
    def _():
        spec[...] += right(other_spec[...], fzh[...], fzl[...]) * twice(turn[...])

    back = right(spec[...], bzh[...], bzl[...])
    real, imag = back[:, 0:256], back[:, 256:512]
    x = jnp.concatenate([jnp.concatenate([real, imag], 1), jnp.concatenate([-imag, real], 1)], 0)
    high, low = split(x)
    x = jnp.concatenate([high, low, high], 0)
    for p in range(3):
        rows = slice(p * 128, p * 128 + 128)
        y = nn(jnp.concatenate([bxh[rows, :], bxh[rows, :], bxl[rows, :]], 1), x)
        to_rows(send2, p, jnp.concatenate([y[:, 0:256], y[:, 256:512]], 0))
        exchange_start(me, p, send2, recv2, ss2, rs2)

    direct_slots(SLOTS // 2, SLOTS, home, other, count, ext, acc)
    back_copy = remote(out_before, returned, back_sem.at[0], back_sem.at[1], below)
    for p in range(3):
        exchange_wait(p, recv2, rs2)
        real, imag = from_rows(recv2, p)
        pot = left(byh[...], byl[...], jnp.concatenate([real, imag], 0))
        grid_to_patches(pot, grid, stacked, p)
    loop(0, ATOM_DEV // SAMPLE, lambda start: sample_chunk(before, start, range(3), stacked, out_before), SAMPLE)
    back_copy.start()
    loop(0, ATOM_DEV // SAMPLE, lambda start: sample_chunk(own, start, range(3), stacked, out), SAMPLE)
    back_copy.wait()
    for c in range(CLU_DEV):
        cols = slice(c * CL, c * CL + CL)
        out[:, cols] += returned[:, cols] + acc[c, 0:3, :]
    for p in range(3):
        exchange_wait(p, send1, ss1)
        exchange_wait(p, send2, ss2)


def on_device(
    positions,
    dipoles,
    spline_values,
    spline_slopes,
    plane_base,
    row_base,
    column_base,
    pair_home,
    pair_other,
    pair_count,
    influence,
):
    constants = [jnp.asarray(t) for t in tables()]
    own = [
        positions,
        dipoles,
        spline_values,
        spline_slopes,
        plane_base.reshape(1, ATOM_DEV),
        row_base.reshape(1, ATOM_DEV),
        column_base.reshape(1, ATOM_DEV),
    ]
    vm = lambda x: pltpu.VMEM(x.shape, x.dtype)
    blocks = pltpu.VMEM((3, DEV, 4, 128), f32)
    return pl.pallas_call(
        kernel,
        out_shape=jax.ShapeDtypeStruct((3, ATOM_DEV), f32),
        in_specs=[SM] * 3 + [VM] * N_ATOM + [pl.BlockSpec(memory_space=pltpu.HBM)] * (1 + N_TABLES),
        out_specs=VM,
        scratch_shapes=[vm(x) for x in own]
        + [vm(x) for x in own[:2]]
        + [vm(x) for x in constants]
        + [pltpu.VMEM((GX, 2, GZ), f32)]
        + [pltpu.VMEM((GX, GZ), f32)] * 4
        + [blocks] * 4
        + [pltpu.VMEM((GX, 512), f32)] * 2
        + [
            pltpu.VMEM((272, 256), f32),
            pltpu.VMEM((48, 8, CL), f32),
            pltpu.VMEM((CLU_DEV, 8, CL), f32),
            pltpu.VMEM((3, ATOM_DEV), f32),
            pltpu.VMEM((3, ATOM_DEV), f32),
        ]
        + [pltpu.VMEM((3, PATCH, 256), f32), pltpu.VMEM((3, PATCH, 512), bf16)]
        + [pltpu.SemaphoreType.DMA((3,))] * 4
        + [pltpu.SemaphoreType.DMA((N_ATOM + 2,))] * 2
        + [pltpu.SemaphoreType.DMA((N_TABLES,)), pltpu.SemaphoreType.DMA]
        + [pltpu.SemaphoreType.DMA((2,))] * 2,
        compiler_params=pltpu.CompilerParams(
            vmem_limit_bytes=62 << 20, collective_id=0, has_side_effects=True
        ),
        name="polarization",
    )(pair_home, pair_other, pair_count, *own, influence, *constants)


def solution(mesh):
    placed = (
        P(None, AXES),
        P(None, AXES),
        P(None, None, AXES),
        P(None, None, AXES),
        P(AXES),
        P(AXES),
        P(AXES),
        P(AXES),
        P(AXES),
        P(AXES),
        P(None, AXES, None),
    )
    return jax.shard_map(
        on_device, mesh=mesh, in_specs=placed, out_specs=P(None, AXES), check_vma=False
    )
```

```python
import functools

import jax
import jax.numpy as jnp
import numpy as np
from jax import lax
from jax.experimental import pallas as pl
from jax.experimental.pallas import tpu as pltpu
from jax.sharding import PartitionSpec as P

CL = 128
CLU_DEV = 16
GX = 384
GY = 256
GZ = 256
DEV = 128
ATOM_DEV = 2048
SLOTS = 32
CHUNK = 1024
SAMPLE = 2048
AXES = ("grp", "sp")

f32, bf16 = jnp.float32, jnp.bfloat16
VM = pl.BlockSpec(memory_space=pltpu.VMEM)
SM = pl.BlockSpec(memory_space=pltpu.SMEM)


def halves(table):
    high = table.astype(bf16)
    low = (table - high.astype(np.float64)).astype(bf16)
    return high, low


@functools.cache
def tables():
    t = np.arange(128)[:, None]
    d = np.where(t < 64, 2 * t, 255 - 2 * t)
    y = np.arange(GY)[None, :]
    angle = 2 * np.pi * ((d * y) % GY) / GY
    real, imag = np.cos(angle), -np.sin(angle)
    imag[0] = 1 - 2 * (np.arange(GY) % 2)
    forward_y = np.concatenate([real, imag], 0)
    scale = np.full((1, 256), 2.0)
    scale[0, 0] = scale[0, 128] = 1.0
    backward_y = forward_y.T * scale / (GX * GY * GZ)
    backward_y = np.concatenate([backward_y, backward_y[:16]], 0)
    z = np.arange(GZ)
    angle = 2 * np.pi * ((z[:, None] * z[None, :]) % GZ) / GZ
    cos, sin = np.cos(angle), np.sin(angle)
    order = 4 * (z % 64) + z // 64
    cos, sin = cos[order], sin[order]
    forward_z = np.block([[cos, -sin], [sin, cos]])
    cos, sin = cos.T, sin.T
    backward_z = np.block([[cos, sin], [-sin, cos]])
    k = np.arange(GX)
    forward_x = []
    for p in range(3):
        angle = 2 * np.pi * ((k[:, None] * (3 * np.arange(128)[None, :] + p)) % GX) / GX
        forward_x += [np.cos(angle), np.sin(angle)]
    backward_x = np.concatenate(
        [np.concatenate([forward_x[2 * p].T, forward_x[2 * p + 1].T], 1) for p in range(3)], 0
    )
    forward_x = np.concatenate(forward_x, 1)
    flip_x = np.eye(GX)[:, -np.arange(GX) % GX]
    flip_z = np.eye(GZ)[:, -np.arange(GZ) % GZ]
    out = [flip_x.astype(bf16), flip_z.astype(bf16)]
    for table in (forward_y, forward_x, forward_z, backward_z, backward_x, backward_y):
        out += list(halves(table))
    return out


def split(x):
    high = x.astype(bf16)
    return high, (x - high.astype(f32)).astype(bf16)


def nn(a, b):
    return lax.dot_general(a, b, (((1,), (0,)), ((), ())), preferred_element_type=f32)


def nt(a, b):
    return lax.dot_general(a, b, (((1,), (1,)), ((), ())), preferred_element_type=f32)


def left(table_high, table_low, x):
    high, low = split(x)
    return nn(
        jnp.concatenate([table_high, table_high, table_low], 1),
        jnp.concatenate([high, low, high], 0),
    )


def right(x, table_high, table_low):
    high, low = split(x)
    return nn(
        jnp.concatenate([high, low, high], 1),
        jnp.concatenate([table_high, table_high, table_low], 0),
    )


FINE_Y, FINE_Z = 72, 7
PATCH = 512


def step_masks(base, n):
    it = lax.broadcasted_iota(jnp.int32, (FINE_Y, n), 0)
    return [it == base + k for k in range(4)]


def one_hot(row, column):
    it = lax.broadcasted_iota(jnp.int32, (256, row.shape[1]), 0)
    return jnp.where(it == (row >> 6) * 64 + (column >> 2), 1.0, 0.0).astype(bf16)


def pick(masks, w):
    r = jnp.where(masks[3], w[3], jnp.zeros((), w[0].dtype))
    for k in (2, 1, 0):
        r = jnp.where(masks[k], w[k], r)
    return r


def plane_weights(local, w, step):
    step = step - local
    r = jnp.zeros_like(w[0])
    for k in range(4):
        r = jnp.where(step == k, w[k], r)
    return r


class Atoms:
    def __init__(self, shift, first, dipoles, values, slopes, plane, row, column):
        self.shift, self.first = shift, first
        self.refs = (dipoles, values, slopes, plane, row, column)

    def read(self, start, n):
        cols = pl.ds(pl.multiple_of(start, n), n)
        dipoles, values, slopes, plane, row, column = self.refs
        m = [dipoles[a : a + 1, cols] for a in range(3)]
        v = [[values[a, k : k + 1, cols] for k in range(4)] for a in range(3)]
        s = [[slopes[a, k : k + 1, cols] for k in range(4)] for a in range(3)]
        return row[:, cols], column[:, cols], plane[:, cols] - self.first, m, v, s


def fine_tables(row, column, v, s):
    at_y = step_masks(row & 63, row.shape[1])
    column = column & 3
    at_z = lambda w: [plane_weights(column, w, f) for f in range(FINE_Z)]
    return pick(at_y, v[1]), pick(at_y, s[1]), at_z(v[2]), at_z(s[2])


def spread_chunk(cell, start, planes, patches):
    row, column, local, m, v, s = cell.read(start, CHUNK)
    v1, s1, v2, s2 = fine_tables(row, column, v, s)
    hot = one_hot(row, column)
    hot = jnp.concatenate([hot, hot], 1)
    for p in planes:
        x0 = plane_weights(local, v[0], p + cell.shift)
        xs = plane_weights(local, s[0], p + cell.shift)
        a = v1 * (m[0] * xs) + s1 * (m[1] * x0)
        b = v1 * (m[2] * x0)
        w = [a * v2[f] + b * s2[f] for f in range(FINE_Z)] + [jnp.zeros((8, CHUNK), f32)]
        high, low = split(jnp.concatenate(w, 0))
        patches[p] += nt(jnp.concatenate([high, low], 1), hot)


def roll_columns(x, step):
    lane = lax.broadcasted_iota(jnp.int32, (x.shape[0], 128), 1) & 63
    out = []
    for h in range(2):
        part = x[:, h * 128 : h * 128 + 128]
        wrapped = lane == (0 if step == 1 else 63)
        out.append(
            jnp.where(
                wrapped, pltpu.roll(part, 65 if step == 1 else 63, 1), pltpu.roll(part, step % 128, 1)
            )
        )
    return jnp.concatenate(out, 1)


def swap_parts(blocks):
    first = lax.broadcasted_iota(jnp.int32, (blocks[0].shape[0], 128), 1) < 64
    half = [[x[:, h * 128 : h * 128 + 128] for h in range(2)] for x in blocks]
    turned = [[pltpu.roll(x, 64, 1) for x in pair] for pair in half]
    out = []
    for part in range(4):
        h, odd = part // 2, part % 2
        row = []
        for g in range(2):
            even_block, odd_block = 2 * g, 2 * g + 1
            if odd:
                row.append(jnp.where(first, turned[even_block][h], half[odd_block][h]))
            else:
                row.append(jnp.where(first, half[even_block][h], turned[odd_block][h]))
        out.append(jnp.concatenate(row, 1))
    return out


def patches_to_grid(patches, p, grid):
    t = [patches[p, f * FINE_Y : f * FINE_Y + FINE_Y, :] for f in range(FINE_Z)]
    t = [t[f] + roll_columns(t[f + 4], 1) if f < 3 else t[f] for f in range(4)]
    grid[...] = jnp.zeros_like(grid)
    for yb, x in enumerate(swap_parts(t)):
        grid[64 * yb : 64 * yb + FINE_Y, :] += x
    grid[0:8, :] += grid[256:264, :]
    return grid[0:256, :]


def grid_to_patches(pot, grid, stacked, p):
    grid[...] = pot
    t = swap_parts([grid[64 * yb : 64 * yb + FINE_Y, :] for yb in range(4)])
    t = t + [roll_columns(t[f], -1) for f in range(3)] + [jnp.zeros((8, 256), f32)]
    high, low = split(jnp.concatenate(t, 0))
    stacked[p] = jnp.concatenate([high, low], 1)


def sample_chunk(cell, start, planes, stacked, out):
    row, column, local, m, v, s = cell.read(start, SAMPLE)
    v1, s1, v2, s2 = fine_tables(row, column, v, s)
    hot = one_hot(row, column)
    hot = jnp.concatenate([hot, hot], 0)
    total = jnp.zeros((3, SAMPLE), f32)
    for p in planes:
        x0 = plane_weights(local, v[0], p + cell.shift)
        xs = plane_weights(local, s[0], p + cell.shift)
        t = nn(stacked[p], hot)
        tv = ts = 0.0
        for f in range(FINE_Z):
            part = t[f * FINE_Y : f * FINE_Y + FINE_Y]
            tv, ts = tv + part * v2[f], ts + part * s2[f]
        r = [
            xs * jnp.sum(v1 * tv, 0, keepdims=True),
            x0 * jnp.sum(s1 * tv, 0, keepdims=True),
            x0 * jnp.sum(v1 * ts, 0, keepdims=True),
        ]
        total = total + jnp.concatenate(r, 0)
    out[:, pl.ds(pl.multiple_of(start, SAMPLE), SAMPLE)] -= total


def extend(parts, ext):
    for part, (positions, dipoles) in enumerate(parts):
        for c in range(CLU_DEV):
            cols = slice(c * CL, c * CL + CL)
            x = positions[:, cols]
            if part != 1:
                shift = 2.0 * (part - 1)
                x = x + jnp.where(lax.broadcasted_iota(jnp.int32, (3, CL), 0) == 0, shift, 0.0)
            ext[part * CLU_DEV + c, 0:3, :] = x
            ext[part * CLU_DEV + c, 3:6, :] = dipoles[:, cols]


def direct_slots(lo, hi, home, other, count, ext, acc):
    eye = (
        lax.broadcasted_iota(jnp.int32, (CL, CL), 0) == lax.broadcasted_iota(jnp.int32, (CL, CL), 1)
    ).astype(f32)
    which = lax.broadcasted_iota(jnp.int32, (CLU_DEV, 8, CL), 0)

    def slot(t, carry):
        h, o = home[t], other[t]
        hx = ext[h + CLU_DEV]
        ox = ext[o].T
        delta = [hx[a : a + 1, :] - ox[:, a : a + 1] for a in range(3)]
        m = [ox[:, 3 + a : 4 + a] for a in range(3)]
        q = delta[0] * delta[0] + delta[1] * delta[1] + delta[2] * delta[2]
        inverse = lax.rsqrt(q + 0.25)
        square = inverse * inverse
        self_slot = jnp.where(o == h + CLU_DEV, 1.0, 0.0)
        first = jnp.exp(-0.5 * q) * (inverse * square) * (1.0 - self_slot * eye)
        second = 3.0 * first * square
        along = second * (delta[0] * m[0] + delta[1] * m[1] + delta[2] * m[2])
        e = [jnp.sum(along * delta[a] - first * m[a], 0, keepdims=True) for a in range(3)]
        live = jnp.where(t < count[0], 0.125, 0.0)
        e = jnp.concatenate(e + [jnp.zeros((5, CL), f32)], 0) * live
        acc[...] += jnp.where(which == h, e[None], 0.0)
        return carry

    lax.fori_loop(lo, hi, slot, 0, unroll=4)


def device_id(t):
    return (t >> 6, t & 63)


def remote(src, dst, send_sem, recv_sem, t):
    return pltpu.make_async_remote_copy(
        src_ref=src,
        dst_ref=dst,
        send_sem=send_sem,
        recv_sem=recv_sem,
        device_id=device_id(t),
        device_id_type=pl.DeviceIdType.MESH,
    )


def exchange_start(me, p, src, dst, send_sem, recv_sem):
    def send(i, c):
        t = (me + i) & (DEV - 1)
        remote(src.at[p, t], dst.at[p, me], send_sem.at[p], recv_sem.at[p], t).start()
        return c

    lax.fori_loop(1, DEV, send, 0, unroll=16)
    dst[p, pl.ds(me, 1)] = src[p, pl.ds(me, 1)]


def exchange_wait(p, src, sem):
    part = src.at[p, pl.ds(0, DEV - 1)]
    pltpu.make_async_copy(part, part, sem.at[p]).wait()


def to_rows(ref, p, value):
    view = ref.at[p].reshape(512, 128)
    for c in range(2):
        for h in range(2):
            view[pl.ds(2 * c + h, 128, stride=4), :] = value[
                c * 128 : c * 128 + 128, h * 128 : h * 128 + 128
            ]


def from_rows(ref, p):
    view = ref.at[p].reshape(512, 128)
    part = [view[pl.ds(k, 128, stride=4), :] for k in range(4)]
    return jnp.concatenate(part[0:2], 1), jnp.concatenate(part[2:4], 1)


def flipped(x, flip_x, flip_z):
    high, low = split(x)
    y = nn(flip_x, jnp.concatenate([high, low], 1))
    high, low = split(y[:, 0:GZ] + y[:, GZ:])
    y = nn(jnp.concatenate([high, low], 0), flip_z)
    return y[0:GX] + y[GX:]


N_TABLES = 14
N_ATOM = 7


def kernel(*refs):
    refs = list(refs)
    take = lambda n: [refs.pop(0) for _ in range(n)]
    home, other, count = take(3)
    own_refs = take(N_ATOM)
    influence, *table_hbm = take(1 + N_TABLES)
    (out,) = take(1)
    before_refs = take(N_ATOM)
    after_refs = take(2)
    table = take(N_TABLES)
    rows_in, sent, got, keep, turn = take(5)
    send1, recv1, send2, recv2, spec, other_spec, grid, ext, acc, out_before, returned = take(11)
    patches, stacked = take(2)
    ss1, rs1, ss2, rs2, atom_ss, atom_rs, table_sem, rows_sem, infl_sem, back_sem = take(10)

    me = lax.axis_index("grp") * 64 + lax.axis_index("sp")
    above, below = lax.rem(me + 1, DEV), lax.rem(me + DEV - 1, DEV)
    loads = [
        pltpu.make_async_copy(a, b, table_sem.at[i])
        for i, (a, b) in enumerate(zip(table_hbm, table))
    ]
    rows_load = pltpu.make_async_copy(influence, rows_in, rows_sem)
    rows_load.start()
    for load in loads:
        load.start()
    barrier = pltpu.get_barrier_semaphore()

    def greet(i, c):
        pl.semaphore_signal(
            barrier,
            inc=1,
            device_id=device_id((me + i) & (DEV - 1)),
            device_id_type=pl.DeviceIdType.MESH,
        )
        return c

    lax.fori_loop(1, DEV, greet, 0, unroll=16)
    own = Atoms(0, 3 * me, *own_refs[1:])
    before = Atoms(3, 3 * below, *before_refs[1:])
    chunks = ATOM_DEV // CHUNK

    def loop(lo, hi, f, n=CHUNK):
        def step(i, c):
            f(i * n)
            return c

        lax.fori_loop(lo, hi, step, 0)

    patches[...] = jnp.zeros_like(patches)
    out[...] = jnp.zeros_like(out)
    out_before[...] = jnp.zeros_like(out_before)
    acc[...] = jnp.zeros_like(acc)
    ext[...] = jnp.zeros_like(ext)
    loop(0, chunks // 2, lambda start: spread_chunk(own, start, range(3), patches))

    pl.semaphore_wait(barrier, DEV - 1)
    copies = [
        remote(a, b, atom_ss.at[i], atom_rs.at[i], above)
        for i, (a, b) in enumerate(zip(own_refs, before_refs))
    ]
    copies += [
        remote(a, b, atom_ss.at[N_ATOM + i], atom_rs.at[N_ATOM + i], below)
        for i, (a, b) in enumerate(zip(own_refs[:2], after_refs))
    ]
    for copy in copies:
        copy.start()
    rows_load.wait()
    lower = me < 64
    sent[...] = jnp.where(lower, rows_in[:, 1, :], rows_in[:, 0, :])
    target = jnp.where(lower, 127 - me, lax.rem(DEV - me, 64))
    infl_copy = remote(sent, got, infl_sem.at[0], infl_sem.at[1], target)
    infl_copy.start()

    loop(chunks // 2, chunks, lambda start: spread_chunk(own, start, range(3), patches))
    for copy in copies:
        copy.wait()
    for load in loads:
        load.wait()
    flip_x, flip_z, fyh, fyl, fxh, fxl, fzh, fzl, bzh, bzl, bxh, bxl, byh, byl = table
    loop(0, chunks, lambda start: spread_chunk(before, start, range(3), patches))
    for p in range(3):
        to_rows(send1, p, left(fyh[...], fyl[...], patches_to_grid(patches, p, grid)))
        exchange_start(me, p, send1, recv1, ss1, rs1)

    extend(
        ((before_refs[0], before_refs[1]), (own_refs[0], own_refs[1]), (after_refs[0], after_refs[1])), ext
    )
    direct_slots(0, SLOTS // 2, home, other, count, ext, acc)
    infl_copy.wait()
    kept = jnp.where(lower, rows_in[:, 0, :], rows_in[:, 1, :])
    u, v = jnp.where(lower, kept, got[...]), jnp.where(lower, got[...], kept)
    same, turned = 0.5 * u, 0.5 * v
    both = 0.25 * (u + v)
    first = me == 0
    keep[...] = jnp.where(first, both, same) + flipped(
        jnp.where(first, both, turned), flip_x[...], flip_z[...]
    )

    @pl.when(first)
    def _():
        q = 0.25 * (rows_in[:, 0, :] - got[...])
        turn[...] = q + flipped(q, flip_x[...], flip_z[...])

    for p in range(3):
        exchange_wait(p, recv1, rs1)
        cols = slice(p * 256, p * 256 + 256)

        real, imag = from_rows(recv1, p)
        x = jnp.concatenate([jnp.concatenate([real, imag], 1), jnp.concatenate([imag, -real], 1)], 0)
        part = left(fxh[:, cols], fxl[:, cols], x)
        if p == 0:
            spec[...] = part
        else:
            spec[...] += part

    twice = lambda x: jnp.concatenate([x, x], 1)
    other_spec[...] = right(spec[...], fzh[...], fzl[...])
    spec[...] = other_spec[...] * twice(keep[...])

    @pl.when(first)
    def _():
        real = flipped(other_spec[:, 0:GZ], flip_x[...], flip_z[...])
        imag = flipped(other_spec[:, GZ:], flip_x[...], flip_z[...])
        spec[...] += jnp.concatenate([real, -imag], 1) * twice(turn[...])

    back = right(spec[...], bzh[...], bzl[...])
    real, imag = back[:, 0:256], back[:, 256:512]
    x = jnp.concatenate([jnp.concatenate([real, imag], 1), jnp.concatenate([-imag, real], 1)], 0)
    high, low = split(x)
    x = jnp.concatenate([high, low, high], 0)
    for p in range(3):
        rows = slice(p * 128, p * 128 + 128)
        y = nn(jnp.concatenate([bxh[rows, :], bxh[rows, :], bxl[rows, :]], 1), x)
        to_rows(send2, p, jnp.concatenate([y[:, 0:256], y[:, 256:512]], 0))
        exchange_start(me, p, send2, recv2, ss2, rs2)

    direct_slots(SLOTS // 2, SLOTS, home, other, count, ext, acc)
    back_copy = remote(out_before, returned, back_sem.at[0], back_sem.at[1], below)
    for p in range(3):
        exchange_wait(p, recv2, rs2)
        real, imag = from_rows(recv2, p)
        pot = left(byh[...], byl[...], jnp.concatenate([real, imag], 0))
        grid_to_patches(pot, grid, stacked, p)
    loop(0, ATOM_DEV // SAMPLE, lambda start: sample_chunk(before, start, range(3), stacked, out_before), SAMPLE)
    back_copy.start()
    loop(0, ATOM_DEV // SAMPLE, lambda start: sample_chunk(own, start, range(3), stacked, out), SAMPLE)
    back_copy.wait()
    for c in range(CLU_DEV):
        cols = slice(c * CL, c * CL + CL)
        out[:, cols] += returned[:, cols] + acc[c, 0:3, :]
    for p in range(3):
        exchange_wait(p, send1, ss1)
        exchange_wait(p, send2, ss2)


def on_device(
    positions,
    dipoles,
    spline_values,
    spline_slopes,
    plane_base,
    row_base,
    column_base,
    pair_home,
    pair_other,
    pair_count,
    influence,
):
    constants = [jnp.asarray(t) for t in tables()]
    own = [
        positions,
        dipoles,
        spline_values,
        spline_slopes,
        plane_base.reshape(1, ATOM_DEV),
        row_base.reshape(1, ATOM_DEV),
        column_base.reshape(1, ATOM_DEV),
    ]
    vm = lambda x: pltpu.VMEM(x.shape, x.dtype)
    blocks = pltpu.VMEM((3, DEV, 4, 128), f32)
    return pl.pallas_call(
        kernel,
        out_shape=jax.ShapeDtypeStruct((3, ATOM_DEV), f32),
        in_specs=[SM] * 3 + [VM] * N_ATOM + [pl.BlockSpec(memory_space=pltpu.HBM)] * (1 + N_TABLES),
        out_specs=VM,
        scratch_shapes=[vm(x) for x in own]
        + [vm(x) for x in own[:2]]
        + [vm(x) for x in constants]
        + [pltpu.VMEM((GX, 2, GZ), f32)]
        + [pltpu.VMEM((GX, GZ), f32)] * 4
        + [blocks] * 4
        + [pltpu.VMEM((GX, 512), f32)] * 2
        + [
            pltpu.VMEM((272, 256), f32),
            pltpu.VMEM((48, 8, CL), f32),
            pltpu.VMEM((CLU_DEV, 8, CL), f32),
            pltpu.VMEM((3, ATOM_DEV), f32),
            pltpu.VMEM((3, ATOM_DEV), f32),
        ]
        + [pltpu.VMEM((3, PATCH, 256), f32), pltpu.VMEM((3, PATCH, 512), bf16)]
        + [pltpu.SemaphoreType.DMA((3,))] * 4
        + [pltpu.SemaphoreType.DMA((N_ATOM + 2,))] * 2
        + [pltpu.SemaphoreType.DMA((N_TABLES,)), pltpu.SemaphoreType.DMA]
        + [pltpu.SemaphoreType.DMA((2,))] * 2,
        compiler_params=pltpu.CompilerParams(
            vmem_limit_bytes=62 << 20, collective_id=0, has_side_effects=True
        ),
        name="polarization",
    )(pair_home, pair_other, pair_count, *own, influence, *constants)


def solution(mesh):
    placed = (
        P(None, AXES),
        P(None, AXES),
        P(None, None, AXES),
        P(None, None, AXES),
        P(AXES),
        P(AXES),
        P(AXES),
        P(AXES),
        P(AXES),
        P(AXES),
        P(None, AXES, None),
    )
    return jax.shard_map(
        on_device, mesh=mesh, in_specs=placed, out_specs=P(None, AXES), check_vma=False
    )
```
